512 devices in a mesh: oy: 8 (over z), ox: 8 (over y_hi, core), ori: 8 (over y_lo, x).
Axes of the slice: x: 4, y: 8 (y_hi: 4, y_lo: 2; y = y_hi * 2 + y_lo), z: 8, core: 2. Of those that a mesh axis runs over, the one named last changes fastest.
Arguments:
- micrograph: float32 [2048, 2048], P('oy', 'ox'), may hold values from -150 to 151
- projections: bfloat16 [64, 192, 192], P(('ox', 'ori')), may hold values from -0.0036315918 to 0.0067443848
- orientations: int32 [16], P('ori'), may hold values from 0 to 63
Outputs:
- best_score: float32 [2048, 2048], P(('oy', 'ori'), 'ox')
- mean_score: float32 [2048, 2048], P(('oy', 'ori'), 'ox')
- mean_square: float32 [2048, 2048], P(('oy', 'ori'), 'ox')
The draws below stay inside these ranges and needn't reach their ends.
All inputs are finite; a program needn't handle non-finite values.
Results may differ from the reference program's by a relative error of at most 0.0003.
Values may be sent and summed in bfloat16 or wider, within the bound.
A program may use at most 64 MiB of HBM per device.

```python
import jax
import jax.numpy as jnp
from jax import lax

P_SIZE = 192
NY = 2048
NX = 2048
ORI = 16
BANK = 64


def draw_micrograph(key, part):
    key = jax.random.fold_in(key, 7)
    row_key, col_key, speckle_key = jax.random.split(key, 3)
    row_scale = jnp.exp(jax.random.uniform(row_key, (NY, 1), jnp.float32, 0.0, 1.15))
    col_scale = jnp.exp(jax.random.uniform(col_key, (1, NX), jnp.float32, 0.0, 1.15))
    gradient = 1.0 + 2.0 * jnp.arange(NY, dtype=jnp.float32)[:, None] / NY
    speckle = jnp.clip(jax.random.normal(speckle_key, (NY, NX), jnp.float32), -5.0, 5.0)
    background = 0.5
    return background + gradient * row_scale * col_scale * speckle


def touch_ends(values, rng, low, high):
    dims = values.shape
    spot = [jax.random.randint(jax.random.fold_in(rng, axis), (), 0, dims[axis]) for axis in range(len(dims))]
    values = values.at[tuple(spot)].set(low)
    longest = dims.index(max(dims))
    spot[longest] = (spot[longest] + 1) % dims[longest]
    return values.at[tuple(spot)].set(high)


def shard_levels(rng, shape, shards, least, largest):
    factor_of, own = 1.0, jax.random.fold_in(rng, 6)
    for axis_at, shards_of in shards:
        steps = jnp.exp(jax.random.uniform(jax.random.fold_in(own, axis_at), (shards_of,), jnp.float32, least / len(shards), largest / len(shards)))
        factor_of = factor_of * jnp.repeat(steps, shape[axis_at] // shards_of).reshape([-1 if axis == axis_at else 1 for axis in range(len(shape))])
    return factor_of


def setup_inputs(seed: int = 0) -> dict:
    splits = jax.random.split(jax.random.key(seed), 4)
    return {
        "micrograph": draw_micrograph(jax.random.fold_in(splits[3], 71), 0),
        "projections": jnp.clip(-0.0036315918 + 0.010375977 * jax.random.uniform(splits[1], (BANK, P_SIZE, P_SIZE), jnp.float32) ** shard_levels(splits[1], (BANK, P_SIZE, P_SIZE), ((0, 64),), -0.2, 0.2), -0.0036315918, 0.0067443848).astype(jnp.bfloat16),
        "orientations": touch_ends(jax.random.randint(splits[2], (ORI,), 0, BANK), jax.random.fold_in(splits[2], 1), 0, BANK - 1).astype(jnp.int32),
    }


def reference(micrograph, projections, orientations):
    cell_count = NY * NX
    image_mean = jnp.sum(micrograph) / cell_count
    centered = micrograph - image_mean
    spread = jnp.sqrt(jnp.sum(centered * centered) / cell_count + 1e-06)
    normed = centered / spread
    padded = jnp.pad(normed, P_SIZE // 2)
    rows_full = NY + P_SIZE
    cols_full = NX + P_SIZE
    image_hat = jnp.fft.rfft2(padded)

    def accumulate(running, entry_id):
        template = projections[entry_id].astype(jnp.float32)
        template_hat = jnp.fft.rfft2(template, s=(rows_full, cols_full))
        correlation = jnp.fft.irfft2(image_hat * jnp.conj(template_hat), s=(rows_full, cols_full))[:NY, :NX]
        highest, summed, squared = running
        return ((jnp.maximum(highest, correlation), summed + correlation, squared + correlation * correlation), None)
    initial = (jnp.full((NY, NX), -jnp.inf, jnp.float32), jnp.zeros((NY, NX), jnp.float32), jnp.zeros((NY, NX), jnp.float32))
    (highest, summed, squared), _ = lax.scan(accumulate, initial, orientations)
    return (highest, summed / ORI, squared / ORI)
```

```python
import functools
import math

import jax
import jax.numpy as jnp
import ml_dtypes
import numpy as np
from jax import lax
from jax.experimental import pallas as pl
from jax.experimental.pallas import tpu as pltpu
from jax.sharding import PartitionSpec as P

MESH = pl.DeviceIdType.MESH
BF16 = jnp.bfloat16
F32 = jnp.float32

TILE = 256
BOX = 192
HALF = 96
LEN = 448
FOLD = LEN // 2
PART = 48
BAND = 32
FREQS = LEN // 2 + 1


def trig(rows, cols):
    turns = np.outer(rows, cols) % LEN
    phase = turns * (2.0 * math.pi / LEN)
    return np.cos(phase), np.sin(phase)


def hi_lo(table):
    table = table.astype(np.float32)
    high = table.astype(ml_dtypes.bfloat16)
    low = (table - high.astype(np.float32)).astype(ml_dtypes.bfloat16)
    return np.stack([high, low])


def tables():
    freq = np.arange(256)
    live = freq < FREQS

    def by_tile(re_part, im_part, axis):
        re_lo, re_hi = np.split(re_part, 2, axis)
        im_lo, im_hi = np.split(im_part, 2, axis)
        return np.concatenate([re_lo, im_lo, re_hi, im_hi], axis)

    lane = np.arange(512)
    place = np.where(lane < 352, lane, lane - 64)
    used = (lane < 352) | (lane >= 416)
    cosine, sine = trig(place, freq)
    keep = used[:, None] & live[None, :]
    image_x = by_tile(cosine * keep, -sine * keep, 1)

    near = np.arange(FOLD)
    image_y = np.stack(
        [np.concatenate(trig(2 * near + odd, near), 0) for odd in (0, 1)]
    )

    column = np.arange(256)
    cosine, sine = trig(column - HALF, freq)
    keep = (column < BOX)[:, None] & live[None, :]
    box_x = by_tile(cosine * keep, -sine * keep, 1)

    order = np.concatenate([2 * near, 2 * near + 1])
    box_y = np.concatenate(trig(order, np.arange(BOX) - HALF), 0)

    pixel = np.arange(TILE)
    back_y = np.concatenate(trig(pixel, order), 0)

    cosine, sine = trig(freq, pixel)
    share = np.where((freq == 0) | (freq == FREQS - 1), 1.0, 2.0) * live / (LEN * LEN)
    back_x = by_tile(cosine * share[:, None], -sine * share[:, None], 0)
    return [hi_lo(t) for t in (image_x, image_y, box_x, box_y, back_y, back_x)]


def split(values):
    high = values.astype(BF16)
    return high, (values - high.astype(F32)).astype(BF16)


def mul(left, right):
    return jnp.dot(left, right, preferred_element_type=F32)


def triple(left_hi, left_lo, right_hi, right_lo):
    return mul(left_hi, right_hi) + (mul(left_hi, right_lo) + mul(left_lo, right_hi))


def kernel(
    x_ref, t_ref, o_ref, ix_h, iy_h, bx_h, by_h, ky_h, kx_h,
    best_ref, mean_ref, square_ref,
    ext, ext_hi, ext_lo, own, bank, mine, some, piece, boxes,
    stat_a, stats_a, stat_b, stats_b, image, corr, got,
    ix, iy, bx, by, ky, kx,
    table_sem, halo_s, halo_r, bank_s, bank_r, some_s, some_r, box_s, box_r, pair_s, pair_r,
    sa_s, sa_r, sb_s, sb_r, out_s, out_r,
):
    z = lax.axis_index("oy")
    a = lax.axis_index("ox")
    j = lax.axis_index("ori")
    core = lax.rem(a, 2)
    chip = a // 2
    partner = a + 1 - 2 * core

    def up(v, d):
        return lax.rem(v + d, 8)

    ori_peers = [{"ori": up(j, d)} for d in range(1, 8)]
    pair_peers = [{"ox": partner, "ori": up(j, d)} for d in range(8)]
    oy_peers = [{"oy": up(z, d)} for d in range(1, 8)]
    ox_peers = [{"ox": up(a, d)} for d in range(1, 8)]
    hi_peers = [{"ox": up(a, 2 * d)} for d in range(1, 4)]
    corner_peers = [{"oy": up(z, dz), "ox": up(a, da)} for dz in (1, 7) for da in (1, 7)]

    barrier = pltpu.get_barrier_semaphore()
    greeted = corner_peers + oy_peers + ox_peers + pair_peers[1:] + ori_peers
    for peer in greeted:
        pl.semaphore_signal(barrier, inc=1, device_id=peer, device_id_type=MESH)

    loads = [
        pltpu.make_async_copy(src, dst, table_sem.at[k])
        for k, (src, dst) in enumerate(
            ((ix_h, ix), (iy_h, iy), (bx_h, bx), (by_h, by), (ky_h, ky), (kx_h, kx))
        )
    ]
    for load in loads:
        load.start()

    own[0] = t_ref[0, :, 0:128]
    own[1] = jnp.zeros((BOX, 128), BF16)
    own[1, :, 0 : BOX - 128] = t_ref[0, :, 128:BOX]

    pixels = x_ref[...]
    count = float(TILE * TILE)
    tile_mean = jnp.sum(jnp.sum(pixels, 0, keepdims=True), 1, keepdims=True) / count
    off = pixels - tile_mean
    tile_dev = jnp.sum(jnp.sum(off * off, 0, keepdims=True), 1, keepdims=True)
    row = lax.broadcasted_iota(jnp.int32, (8, 128), 0)
    stat_a[...] = jnp.where(row == 0, tile_mean, tile_dev)

    pl.semaphore_wait(barrier, len(greeted))

    def send(src, dst, s, r, peer):
        copy = pltpu.make_async_remote_copy(
            src_ref=src, dst_ref=dst, send_sem=s, recv_sem=r, device_id=peer, device_id_type=MESH
        )
        copy.start()
        return copy

    strip = lax.rem(z, 4)
    lanes = z // 4
    strip_rows = pl.ds(pl.multiple_of(strip * PART, 16), PART)
    bank_copies = [
        send(own.at[lanes, strip_rows], bank.at[k], bank_s.at[k], bank_r.at[k], peer)
        for k, peer in enumerate(ori_peers + pair_peers)
    ]
    stat_a_copies = [
        send(stat_a, stats_a.at[k], sa_s.at[k], sa_r.at[k], peer) for k, peer in enumerate(oy_peers)
    ]
    row_kind = {0: (0, 256, 0), 7: (0, HALF, 256), 1: (TILE - HALF, HALF, 352)}
    col_kind = {0: (0, 256, 0), 7: (0, 128, 256), 1: (128, 128, 384)}
    halo_copies = []
    for dz in (0, 1, 7):
        for da in (0, 1, 7):
            if dz == 0 and da == 0:
                continue
            r_from, r_size, r_to = row_kind[dz]
            c_from, c_size, c_to = col_kind[da]
            k = len(halo_copies)
            halo_copies.append(
                send(
                    x_ref.at[pl.ds(r_from, r_size), pl.ds(c_from, c_size)],
                    ext.at[pl.ds(r_to, r_size), pl.ds(c_to, c_size)],
                    halo_s.at[k], halo_r.at[k], {"oy": up(z, dz), "ox": up(a, da)},
                )
            )

    want = o_ref[core]
    local = own[lanes, strip_rows, :].astype(F32)
    total = jnp.where(a * 8 + j == want, 1.0, 0.0) * local
    for k, copy in enumerate(bank_copies):
        copy.wait()
        d = k + 1 if k < 7 else k - 7
        column = a if k < 7 else partner
        entry = column * 8 + lax.rem(j + 8 - d, 8)
        total += jnp.where(entry == want, 1.0, 0.0) * bank[k].astype(F32)
    mine[...] = total.astype(BF16)
    some_copies = [
        send(mine, some.at[k], some_s.at[k], some_r.at[k], peer) for k, peer in enumerate(hi_peers)
    ]

    def merge(first, others, number):
        means = [first[0:1, :]] + [others[k, 0:1, :] for k in range(7)]
        devs = [first[1:2, :]] + [others[k, 1:2, :] for k in range(7)]
        mid = sum(means) * 0.125
        dev = sum(devs) + number * sum((m - mid) * (m - mid) for m in means)
        return mid, dev

    for copy in stat_a_copies:
        copy.wait()
    mid, dev = merge(stat_a, stats_a, count)
    stat_b[...] = jnp.where(row == 0, mid, dev)
    stat_b_copies = [
        send(stat_b, stats_b.at[k], sb_s.at[k], sb_r.at[k], peer) for k, peer in enumerate(ox_peers)
    ]

    total = mine[...].astype(F32)
    for k, copy in enumerate(some_copies):
        copy.wait()
        total += some[k].astype(F32)
    piece[...] = total.astype(BF16)
    box_copies = [
        send(piece, boxes.at[0, lanes, strip_rows], box_s.at[k], box_r.at[k], peer)
        for k, peer in enumerate(oy_peers)
    ]
    boxes[0, lanes, strip_rows, :] = piece[...]

    for copy in stat_b_copies:
        copy.wait()
    mid, dev = merge(stat_b, stats_b, count * 8)
    scale = 1.0 / jnp.sqrt(dev / (count * 64) + 1e-06)
    mid, scale = mid[:, 0:1], scale[:, 0:1]
    for copy in halo_copies:
        copy.wait()
    for r_at, r_size, r_ok in ((0, 256, None), (256, HALF, z < 7), (352, HALF, z > 0)):
        for c_at, c_size, c_ok in ((0, 256, None), (256, 128, a < 7), (384, 128, a > 0)):
            inside = scale
            for ok in (r_ok, c_ok):
                if ok is not None:
                    inside = inside * jnp.where(ok, 1.0, 0.0)
            if r_at == 0 and c_at == 0:
                values = pixels
            else:
                values = ext[r_at : r_at + r_size, c_at : c_at + c_size]
            high, low = split((values - mid) * inside)
            ext_hi[r_at : r_at + r_size, c_at : c_at + c_size] = high
            ext_lo[r_at : r_at + r_size, c_at : c_at + c_size] = low

    for load in loads:
        load.wait()

    def rotate(both, size):
        low, high = both[:size], both[size:]
        return jnp.concatenate(
            [low[:, :128] + high[:, 128:], low[:, 128:] - high[:, :128]], axis=1
        )

    def image_tile(tau, _):
        at = pl.ds(pl.multiple_of(tau * 256, 256), 256)
        lines = triple(ext_hi[...], ext_lo[...], ix[0, :, at], ix[1, :, at])
        upper, lower = lines[:FOLD], lines[FOLD:]
        for odd, folded in ((0, upper + lower), (1, upper - lower)):
            high, low = split(folded)
            both = triple(iy[0, odd], iy[1, odd], high, low)
            image[pl.ds(odd * FOLD, FOLD), at] = rotate(both, FOLD)
        return _

    lax.fori_loop(0, 2, image_tile, 0)

    for copy in box_copies:
        copy.wait()
    pair_copy = send(boxes.at[0], boxes.at[1], pair_s, pair_r, {"ox": partner})

    out_copies = []
    for slot in range(2):
        if slot == 1:
            pair_copy.wait()
        box = jnp.concatenate([boxes[slot, 0], boxes[slot, 1]], axis=1)

        def slot_tile(tau, _, box=box, slot=slot):
            at = pl.ds(pl.multiple_of(tau * 256, 256), 256)
            high, low = split(mul(box, bx[0, :, at]) + mul(box, bx[1, :, at]))
            wave = rotate(triple(by[0], by[1], high, low), LEN)
            t_re, t_im = wave[:, :128], wave[:, 128:]
            g = image[:, at]
            g_re, g_im = g[:, :128], g[:, 128:]
            joint = jnp.concatenate(
                [g_re * t_re + g_im * t_im, g_im * t_re - g_re * t_im], axis=1
            )
            high, low = split(joint)
            both = triple(ky[0], ky[1], high, low)
            low_half, high_half = both[:TILE], both[TILE:]
            lines = jnp.concatenate(
                [low_half[:, :128] - high_half[:, 128:], low_half[:, 128:] + high_half[:, :128]],
                axis=1,
            )
            high, low = split(lines)
            part = triple(high, low, kx[0, at, :], kx[1, at, :])

            if True:
                corr[slot] = jnp.where(tau == 0, part, corr[slot] + part)
            return _

        corr[slot] = jnp.zeros((TILE, TILE), F32)
        lax.fori_loop(0, 2, slot_tile, 0)
        for d in range(1, 8):
            to = lax.rem(j + d, 8)
            k = slot * 7 + d - 1
            out_copies.append(
                send(
                    corr.at[slot, pl.ds(pl.multiple_of(to * BAND, BAND), BAND)],
                    got.at[k], out_s.at[k], out_r.at[k], {"ori": to},
                )
            )

    band = pl.ds(pl.multiple_of(j * BAND, BAND), BAND)
    one, two = corr[0, band, :], corr[1, band, :]
    best = jnp.maximum(one, two)
    summed = one + two
    squared = one * one + two * two
    for k, copy in enumerate(out_copies):
        copy.wait()
        value = got[k]
        best = jnp.maximum(best, value)
        summed += value
        squared += value * value
    best_ref[...] = best
    mean_ref[...] = summed / 16.0
    square_ref[...] = squared / 16.0


def body(micrograph, projections, orientations):
    consts = tables()
    vmem = pl.BlockSpec(memory_space=pltpu.VMEM)
    hbm = pl.BlockSpec(memory_space=pl.ANY)
    dma = pltpu.SemaphoreType.DMA
    out = jax.ShapeDtypeStruct((BAND, TILE), F32)
    scratch = [
        pltpu.VMEM((LEN, 512), F32),
        pltpu.VMEM((LEN, 512), BF16),
        pltpu.VMEM((LEN, 512), BF16),
        pltpu.VMEM((2, BOX, 128), BF16),
        pltpu.VMEM((15, PART, 128), BF16),
        pltpu.VMEM((PART, 128), BF16),
        pltpu.VMEM((3, PART, 128), BF16),
        pltpu.VMEM((PART, 128), BF16),
        pltpu.VMEM((2, 2, BOX, 128), BF16),
        pltpu.VMEM((8, 128), F32),
        pltpu.VMEM((7, 8, 128), F32),
        pltpu.VMEM((8, 128), F32),
        pltpu.VMEM((7, 8, 128), F32),
        pltpu.VMEM((LEN, 512), F32),
        pltpu.VMEM((2, TILE, TILE), F32),
        pltpu.VMEM((14, BAND, TILE), F32),
    ]
    scratch += [pltpu.VMEM(c.shape, BF16) for c in consts]
    scratch += [dma((6,))]
    for n in (8, 15, 3, 7):
        scratch += [dma((n,)), dma((n,))]
    scratch += [dma, dma]
    for n in (7, 7, 14):
        scratch += [dma((n,)), dma((n,))]
    return pl.pallas_call(
        kernel,
        out_shape=(out, out, out),
        in_specs=[vmem, vmem, pl.BlockSpec(memory_space=pltpu.SMEM)] + [hbm] * 6,
        out_specs=(vmem, vmem, vmem),
        scratch_shapes=scratch,
        name="match",
        compiler_params=pltpu.CompilerParams(
            collective_id=0, has_side_effects=True, vmem_limit_bytes=48 * 1024 * 1024
        ),
    )(micrograph, projections, orientations, *[jnp.asarray(c) for c in consts])


def solution(mesh):
    in_specs = (P("oy", "ox"), P(("ox", "ori"), None, None), P("ori"))
    out_specs = (P(("oy", "ori"), "ox"), P(("oy", "ori"), "ox"), P(("oy", "ori"), "ox"))
    return jax.shard_map(body, mesh=mesh, in_specs=in_specs, out_specs=out_specs, check_vma=False)
```

```python
import functools
import math

import jax
import jax.numpy as jnp
import ml_dtypes
import numpy as np
from jax import lax
from jax.experimental import pallas as pl
from jax.experimental.pallas import tpu as pltpu
from jax.sharding import PartitionSpec as P

MESH = pl.DeviceIdType.MESH
BF16 = jnp.bfloat16
F32 = jnp.float32

TILE = 256
BOX = 192
HALF = 96
LEN = 448
FOLD = LEN // 2
PART = 96
BAND = 32
FREQS = LEN // 2 + 1


def trig(rows, cols):
    turns = np.outer(rows, cols) % LEN
    phase = turns * (2.0 * math.pi / LEN)
    return np.cos(phase), np.sin(phase)


def stacked(table, axis, order):
    table = table.astype(np.float32)
    high = table.astype(ml_dtypes.bfloat16)
    low = (table - high.astype(np.float32)).astype(ml_dtypes.bfloat16)
    return np.concatenate([{"h": high, "l": low}[c] for c in order], axis)


def waves(freqs, places):
    cosine, sine = trig(freqs, places)
    if freqs[0] == 0:
        sine[0] = np.cos(math.pi * places)
    return cosine, sine


def tables():
    freq = np.arange(256)
    live = freq < FREQS

    def by_tile(re_part, im_part, axis):
        re_lo, re_hi = np.split(re_part, 2, axis)
        im_lo, im_hi = np.split(im_part, 2, axis)
        return np.concatenate([re_lo, im_lo, re_hi, im_hi], axis)

    lane = np.arange(512)
    place = np.where(lane < 352, lane, lane - 64)
    used = (lane < 352) | (lane >= 416)
    cosine, sine = trig(place, freq)
    keep = used[:, None] & live[None, :]
    image_x = stacked(by_tile(cosine * keep, -sine * keep, 1), 0, "hhl")

    near = np.arange(FOLD)
    even, odd = np.arange(0, FOLD, 2), np.arange(1, FOLD, 2)
    image_y = stacked(np.stack([np.concatenate(waves(k, near), 0) for k in (even, odd)]), 2, "hhl")

    column = np.arange(256)
    cosine, sine = trig(column - HALF, freq)
    keep = (column < BOX)[:, None] & live[None, :]
    box_x = stacked(by_tile(cosine * keep, -sine * keep, 1), 0, "hl")

    order = np.concatenate([even, odd])
    box_y = stacked(np.concatenate(waves(order, np.arange(BOX) - HALF), 0), 1, "hhl")

    pixel = np.arange(TILE)
    back_y = stacked(np.concatenate([w.T for w in waves(order, pixel)], 1), 1, "hhl")

    cosine, sine = trig(freq, pixel)
    share = np.where((freq == 0) | (freq == FREQS - 1), 1.0, 2.0) * live / (LEN * LEN)
    back_x = by_tile(cosine * share[:, None], -sine * share[:, None], 0)
    back_x = stacked(back_x.reshape(2, 256, TILE), 1, "hhl")
    return [image_x, image_y, box_x, box_y, back_y, back_x]


def split(values):
    high = values.astype(BF16)
    return high, (values - high.astype(F32)).astype(BF16)


def mul(left, right):
    return jnp.dot(left, right, preferred_element_type=F32)


def left_of(values, axis=0):
    high, low = split(values)
    return jnp.concatenate([high, low, high], axis=axis)


def both_ways(both):
    even, odd = both[:FOLD], both[FOLD:]
    first = lax.broadcasted_iota(jnp.int32, even.shape, 0) == 0
    turned = jnp.concatenate([odd[:, 128:], -odd[:, :128]], axis=1)
    plus = even + jnp.where(first, 0.0, turned)
    minus = jnp.where(first, odd, even - turned)
    return plus, minus


def conj_product(g, t):
    g_re, g_im, t_re, t_im = g[:, :128], g[:, 128:], t[:, :128], t[:, 128:]
    return g_re * t_re + g_im * t_im, g_im * t_re - g_re * t_im


def kernel(
    x_ref, t_ref, o_ref, ix_h, iy_h, bx_h, by_h, ky_h, kx_h,
    out_ref,
    pixels_in, box_in, wanted, ext, ext_hi, ext_lo, own, bank, mine, some, piece, boxes,
    stat_a, stats_a, stat_b, stats_b, image, corr, got,
    ix, iy, bx, by, ky, kx,
    own_sem, table_sem, halo_s, halo_r, bank_s, bank_r, some_s, some_r, box_s, box_r,
    down_s, up_s, sa_r, sb_s, sb_r, out_s, out_r,
):
    z = lax.axis_index("oy")
    a = lax.axis_index("ox")
    j = lax.axis_index("ori")
    core = lax.rem(a, 2)
    partner = a + 1 - 2 * core
    half = lax.rem(z, 2)
    beside = z + 1 - 2 * half

    def turn(v, d):
        return lax.rem(v + d, 8)

    ori_peers = [{"ori": turn(j, d)} for d in range(1, 8)]
    pair_peers = [{"ox": partner, "ori": turn(j, d)} for d in range(8)]
    ox_peers = [{"ox": turn(a, d)} for d in range(1, 8)]
    hi_peers = [{"ox": turn(a, 2 * d)} for d in range(1, 4)]
    box_peers = [{"ox": partner}, {"oy": beside}, {"oy": beside, "ox": partner}]

    barrier = pltpu.get_barrier_semaphore()

    def greet(peer):
        pl.semaphore_signal(barrier, inc=1, device_id=peer, device_id_type=MESH)

    sides = ((1, z < 7, z > 0), (-1, z > 0, z < 7))
    for dz, there, _ in sides:

        @pl.when(there)
        def _(dz=dz):
            greet({"oy": z + dz})

    for peer in ox_peers + pair_peers[1:] + ori_peers + box_peers[2:]:
        greet(peer)
    for d in range(2, 8):

        @pl.when(z + d < 8)
        def _(d=d):
            greet({"oy": z + d})

    greetings = (
        22
        + jnp.where(z > 0, 1, 0)
        + jnp.where(z < 7, 1, 0)
        + jnp.where(z > 1, z - 1, 0)
    )

    own_loads = [
        pltpu.make_async_copy(src, dst, own_sem.at[k])
        for k, (src, dst) in enumerate(((x_ref, pixels_in), (t_ref, box_in), (o_ref, wanted)))
    ]
    loads = [
        pltpu.make_async_copy(src, dst, table_sem.at[k])
        for k, (src, dst) in enumerate(
            ((ix_h, ix), (iy_h, iy), (bx_h, bx), (by_h, by), (ky_h, ky), (kx_h, kx))
        )
    ]
    for load in own_loads + loads:
        load.start()
    for load in own_loads:
        load.wait()

    own[0] = box_in[0, :, 0:128]
    own[1] = jnp.zeros((BOX, 128), BF16)
    own[1, :, 0 : BOX - 128] = box_in[0, :, 128:BOX]

    pixels = pixels_in[...]
    count = float(TILE * TILE)
    tile_mean = jnp.sum(jnp.sum(pixels, 0, keepdims=True), 1, keepdims=True) / count
    off = pixels - tile_mean
    tile_dev = jnp.sum(jnp.sum(off * off, 0, keepdims=True), 1, keepdims=True)
    row = lax.broadcasted_iota(jnp.int32, (8, 128), 0)
    stat_a[...] = jnp.where(row == 0, tile_mean, tile_dev)
    stats_a[z] = stat_a[...]

    pl.semaphore_wait(barrier, greetings)

    def copier(src, dst, s, r, peer):
        return pltpu.make_async_remote_copy(
            src_ref=src, dst_ref=dst, send_sem=s, recv_sem=r, device_id=peer, device_id_type=MESH
        )

    def send(*what):
        copy = copier(*what)
        copy.start()
        return copy

    mid_rows = pl.ds(pl.multiple_of(half * PART, 16), PART)
    bank_copies = [
        send(
            own.at[core if k < 7 else 1 - core, mid_rows],
            bank.at[k], bank_s.at[k], bank_r.at[k], peer,
        )
        for k, peer in enumerate(ori_peers + pair_peers)
    ]

    def tell(d, s):
        return copier(stat_a, stats_a.at[z], s.at[abs(d) - 1], sa_r.at[z], {"oy": z + d})

    def heard(d):
        copier(stat_a, stats_a.at[z + d], up_s.at[0], sa_r.at[z + d], {"oy": z + d}).wait_recv()

    for d in range(1, 8):

        @pl.when(z - d >= 0)
        def _(d=d):
            tell(-d, down_s).start()

    row_kind = {-1: (0, 256), 1: (TILE - HALF, 352)}
    across = [
        send(
            pixels_in.at[:, pl.ds(c_from, 128)], ext.at[pl.ds(0, TILE), pl.ds(c_to, 128)],
            halo_s.at[k], halo_r.at[k], {"ox": turn(a, da)},
        )
        for k, (da, c_from, c_to) in enumerate(((1, 128, 384), (7, 0, 256)))
    ]

    def along(k, dz, source, lanes):
        r_from, r_to = row_kind[dz]
        return copier(
            source.at[pl.ds(r_from, HALF), lanes], ext.at[pl.ds(r_to, HALF), lanes],
            halo_s.at[k], halo_r.at[k], {"oy": z + dz},
        )

    def straight(n):
        return along(2 + n, sides[n][0], pixels_in, pl.ds(0, 256))

    def corners(n):
        return along(4 + n, sides[n][0], ext, pl.ds(256, 256))

    for n in range(2):

        @pl.when(sides[n][1])
        def _(n=n):
            straight(n).start()

    totals = []
    for slot in range(2):
        local = own[core, mid_rows, :].astype(F32)
        totals.append(jnp.where(a * 8 + j == wanted[slot], 1.0, 0.0) * local)
    for k, copy in enumerate(bank_copies):
        copy.wait()
        d = k + 1 if k < 7 else k - 7
        column = a if k < 7 else partner
        entry = column * 8 + lax.rem(j + 8 - d, 8)
        arrived = bank[k].astype(F32)
        for slot in range(2):
            totals[slot] += jnp.where(entry == wanted[slot], 1.0, 0.0) * arrived
    some_copies = []
    for slot in range(2):
        mine[slot] = totals[slot].astype(BF16)
        for k, peer in enumerate(hi_peers):
            n = slot * 3 + k
            some_copies.append(send(mine.at[slot], some.at[n], some_s.at[n], some_r.at[n], peer))

    def merge(tiles, number):
        means = [t[0:1, :] for t in tiles]
        mid = sum(means) * 0.125
        dev = sum(t[1:2, :] for t in tiles) + number * sum((m - mid) * (m - mid) for m in means)
        return mid, dev

    for copy in across:
        copy.wait()
    for n in range(2):

        @pl.when(sides[n][1])
        def _(n=n):
            corners(n).start()

    for copy_of in (straight, corners):
        for n in range(2):

            @pl.when(sides[n][1])
            def _(n=n, copy_of=copy_of):
                copy_of(n).wait_send()

            @pl.when(sides[n][2])
            def _(n=n, copy_of=copy_of):
                copy_of(n).wait_recv()

    for r_at, r_size, r_ok in ((0, 256, None), (256, HALF, z < 7), (352, HALF, z > 0)):
        for c_at, c_size, c_ok in ((0, 256, None), (256, 128, a < 7), (384, 128, a > 0)):
            if r_at == 0 and c_at == 0:
                values = pixels_in[...] - tile_mean
            else:
                values = ext[r_at : r_at + r_size, c_at : c_at + c_size] - tile_mean
            for ok in (r_ok, c_ok):
                if ok is not None:
                    values = jnp.where(ok, values, 0.0)
            high, low = split(values)
            ext_hi[r_at : r_at + r_size, c_at : c_at + c_size] = high
            ext_lo[r_at : r_at + r_size, c_at : c_at + c_size] = low

    for load in loads:
        load.wait()

    for tau in range(2):
        at = slice(tau * 256, tau * 256 + 256)
        whole = jnp.concatenate([ext_hi[...], ext_lo[...], ext_hi[...]], axis=1)
        lines = mul(whole, ix[:, at])
        upper, lower = lines[:FOLD], lines[FOLD:]
        even = mul(iy[0], left_of(upper + lower))
        odd = mul(iy[1], left_of(upper - lower))
        quarter = FOLD // 2
        image[0, :, at], image[1, :, at] = both_ways(
            jnp.concatenate([even[:quarter], odd[:quarter], even[quarter:], odd[quarter:]], axis=0)
        )

    for d in range(1, 8):

        @pl.when(z + d < 8)
        def _(d=d):
            heard(d)
            tell(d, up_s).start()

    box_copies = []
    for slot in range(2):
        total = mine[slot].astype(F32)
        for k in range(3):
            some_copies[slot * 3 + k].wait()
            total += some[slot * 3 + k].astype(F32)
        piece[slot] = total.astype(BF16)
        boxes[slot, core, mid_rows, :] = piece[slot]
        for k, peer in enumerate(box_peers):
            n = slot * 3 + k
            box_copies.append(
                send(piece.at[slot], boxes.at[slot, core, mid_rows], box_s.at[n], box_r.at[n], peer)
            )

    for d in range(1, 8):

        @pl.when(z - d >= 0)
        def _(d=d):
            heard(-d)

    mid, dev = merge([stats_a.at[k] for k in range(8)], count)
    stat_b[...] = jnp.where(row == 0, mid, dev)
    stat_copies = [
        send(stat_b, stats_b.at[k], sb_s.at[k], sb_r.at[k], peer) for k, peer in enumerate(ox_peers)
    ]

    y_at = lax.broadcasted_iota(jnp.int32, (TILE, BOX), 0)
    u_at = lax.broadcasted_iota(jnp.int32, (TILE, BOX), 1)
    line = z * TILE + y_at + u_at - HALF
    row_in = jnp.where((line >= 0) & (line < 8 * TILE), 1.0, 0.0).astype(BF16)
    v_at = lax.broadcasted_iota(jnp.int32, (TILE, TILE), 0)
    x_at = lax.broadcasted_iota(jnp.int32, (TILE, TILE), 1)
    line = a * TILE + x_at + v_at - HALF
    col_in = jnp.where((line >= 0) & (line < 8 * TILE), 1.0, 0.0).astype(BF16)

    out_copies = []
    for slot in range(2):
        for k in range(3):
            box_copies[slot * 3 + k].wait()
        box = jnp.concatenate([boxes[slot, 0], boxes[slot, 1]], axis=1)

        twice = jnp.concatenate([box, box], axis=1)
        parts = []
        for tau in range(2):
            at = slice(tau * 256, tau * 256 + 256)
            t_plus, t_minus = both_ways(mul(by[...], left_of(mul(twice, bx[:, at]))))
            p_re, p_im = conj_product(image[0, :, at], t_plus)
            m_re, m_im = conj_product(image[1, :, at], t_minus)
            first = lax.broadcasted_iota(jnp.int32, (FOLD, 128), 0) == 0
            joint = jnp.concatenate(
                [
                    jnp.concatenate(
                        [p_re + jnp.where(first, 0.0, m_re), p_im + jnp.where(first, 0.0, m_im)],
                        axis=1,
                    ),
                    jnp.concatenate(
                        [jnp.where(first, m_re, m_im - p_im), jnp.where(first, m_im, p_re - m_re)],
                        axis=1,
                    ),
                ],
                axis=0,
            )
            parts.append(mul(left_of(mul(ky[...], left_of(joint)), 1), kx[tau]))
        high, low = split(mul(row_in, box))
        cover = mul(high, col_in) + mul(low, col_in)

        if slot == 0:
            for copy in stat_copies:
                copy.wait()
            mid, dev = merge([stat_b] + [stats_b.at[k] for k in range(7)], count * 8)
            scale = 1.0 / jnp.sqrt(dev[:, 0:1] / (count * 64) + 1e-06)
            rest = mid[:, 0:1] - tile_mean
        corr[slot] = parts[0] + parts[1] - rest * cover

        for d in range(1, 8):
            to = turn(j, d)
            k = slot * 7 + d - 1
            out_copies.append(
                send(
                    corr.at[slot, pl.ds(pl.multiple_of(to * BAND, BAND), BAND)],
                    got.at[k], out_s.at[k], out_r.at[k], {"ori": to},
                )
            )

    band = pl.ds(pl.multiple_of(j * BAND, BAND), BAND)
    one, two = corr[0, band, :], corr[1, band, :]
    best = jnp.maximum(one, two)
    summed = one + two
    squared = one * one + two * two
    for k, copy in enumerate(out_copies):
        copy.wait()
        value = got[k]
        best = jnp.maximum(best, value)
        summed += value
        squared += value * value
    out_ref[0] = best * scale
    out_ref[1] = summed * scale
    out_ref[2] = squared * (scale * scale)
    for d in range(1, 8):

        @pl.when(z - d >= 0)
        def _(d=d):
            tell(-d, down_s).wait_send()

        @pl.when(z + d < 8)
        def _(d=d):
            tell(d, up_s).wait_send()


def body(micrograph, projections, orientations):
    consts = tables()
    vmem = pl.BlockSpec(memory_space=pltpu.VMEM)
    hbm = pl.BlockSpec(memory_space=pl.ANY)
    dma = pltpu.SemaphoreType.DMA
    out = jax.ShapeDtypeStruct((3, BAND, TILE), F32)
    scratch = [
        pltpu.VMEM((TILE, TILE), F32),
        pltpu.VMEM((1, BOX, BOX), BF16),
        pltpu.SMEM((2,), jnp.int32),
        pltpu.VMEM((LEN, 512), F32),
        pltpu.VMEM((LEN, 512), BF16),
        pltpu.VMEM((LEN, 512), BF16),
        pltpu.VMEM((2, BOX, 128), BF16),
        pltpu.VMEM((15, PART, 128), BF16),
        pltpu.VMEM((2, PART, 128), BF16),
        pltpu.VMEM((6, PART, 128), BF16),
        pltpu.VMEM((2, PART, 128), BF16),
        pltpu.VMEM((2, 2, BOX, 128), BF16),
        pltpu.VMEM((8, 128), F32),
        pltpu.VMEM((8, 8, 128), F32),
        pltpu.VMEM((8, 128), F32),
        pltpu.VMEM((7, 8, 128), F32),
        pltpu.VMEM((2, FOLD, 512), F32),
        pltpu.VMEM((2, TILE, TILE), F32),
        pltpu.VMEM((14, BAND, TILE), F32),
    ]
    scratch += [pltpu.VMEM(c.shape, BF16) for c in consts]
    for n in (3, 6, 6, 6, 15, 15, 6, 6, 6, 6, 7, 7, 8, 7, 7, 14, 14):
        scratch.append(dma((n,)))
    stats = pl.pallas_call(
        kernel,
        out_shape=out,
        in_specs=[hbm] * 9,
        out_specs=vmem,
        scratch_shapes=scratch,
        name="match",
        compiler_params=pltpu.CompilerParams(
            collective_id=0, has_side_effects=True, vmem_limit_bytes=60 * 1024 * 1024
        ),
    )(micrograph, projections, orientations, *[jnp.asarray(c) for c in consts])
    return stats[0], stats[1] / 16.0, stats[2] / 16.0


def solution(mesh):
    in_specs = (P("oy", "ox"), P(("ox", "ori"), None, None), P("ori"))
    out_specs = (P(("oy", "ori"), "ox"), P(("oy", "ori"), "ox"), P(("oy", "ori"), "ox"))
    return jax.shard_map(body, mesh=mesh, in_specs=in_specs, out_specs=out_specs, check_vma=False)
```

```python
import functools
import math

import jax
import jax.numpy as jnp
import ml_dtypes
import numpy as np
from jax import lax
from jax.experimental import pallas as pl
from jax.experimental.pallas import tpu as pltpu
from jax.sharding import PartitionSpec as P

MESH = pl.DeviceIdType.MESH
BF16 = jnp.bfloat16
F32 = jnp.float32

TILE = 256
BOX = 192
HALF = 96
LEN = 448
FOLD = LEN // 2
PART = 96
BAND = 32
FREQS = LEN // 2 + 1


def trig(rows, cols):
    turns = np.outer(rows, cols) % LEN
    phase = turns * (2.0 * math.pi / LEN)
    return np.cos(phase), np.sin(phase)


def stacked(table, axis, order):
    table = table.astype(np.float32)
    high = table.astype(ml_dtypes.bfloat16)
    low = (table - high.astype(np.float32)).astype(ml_dtypes.bfloat16)
    return np.concatenate([{"h": high, "l": low}[c] for c in order], axis)


def waves(freqs, places):
    cosine, sine = trig(freqs, places)
    if freqs[0] == 0:
        sine[0] = np.cos(math.pi * places)
    return cosine, sine


def tables():
    freq = np.arange(256)
    live = freq < FREQS

    def by_tile(re_part, im_part, axis):
        re_lo, re_hi = np.split(re_part, 2, axis)
        im_lo, im_hi = np.split(im_part, 2, axis)
        return np.concatenate([re_lo, im_lo, re_hi, im_hi], axis)

    lane = np.arange(512)
    place = np.where(lane < 352, lane, lane - 64)
    used = (lane < 352) | (lane >= 416)
    cosine, sine = trig(place, freq)
    keep = used[:, None] & live[None, :]
    image_x = stacked(by_tile(cosine * keep, -sine * keep, 1), 0, "hhl")

    near = np.arange(FOLD)
    even, odd = np.arange(0, FOLD, 2), np.arange(1, FOLD, 2)
    image_y = stacked(np.stack([np.concatenate(waves(k, near), 0) for k in (even, odd)]), 2, "hhl")

    column = np.arange(256)
    cosine, sine = trig(column - HALF, freq)
    keep = (column < BOX)[:, None] & live[None, :]
    box_x = stacked(by_tile(cosine * keep, -sine * keep, 1), 0, "hl")

    order = np.concatenate([even, odd])
    box_y = stacked(np.concatenate(waves(order, np.arange(BOX) - HALF), 0), 1, "hhl")

    pixel = np.arange(TILE)
    back_y = stacked(np.concatenate([w.T for w in waves(order, pixel)], 1), 1, "hhl")

    cosine, sine = trig(freq, pixel)
    share = np.where((freq == 0) | (freq == FREQS - 1), 1.0, 2.0) * live / (LEN * LEN)
    back_x = by_tile(cosine * share[:, None], -sine * share[:, None], 0)
    back_x = stacked(back_x.reshape(2, 256, TILE), 1, "hhl")
    return [image_x, image_y, box_x, box_y, back_y, back_x]


def split(values):
    high = values.astype(BF16)
    return high, (values - high.astype(F32)).astype(BF16)


def mul(left, right):
    return jnp.dot(left, right, preferred_element_type=F32)


def left_of(values, axis=0):
    high, low = split(values)
    return jnp.concatenate([high, low, high], axis=axis)


def both_ways(both):
    even, odd = both[:FOLD], both[FOLD:]
    first = lax.broadcasted_iota(jnp.int32, even.shape, 0) == 0
    turned = jnp.concatenate([odd[:, 128:], -odd[:, :128]], axis=1)
    plus = even + jnp.where(first, 0.0, turned)
    minus = jnp.where(first, odd, even - turned)
    return plus, minus


def conj_product(g, t):
    g_re, g_im, t_re, t_im = g[:, :128], g[:, 128:], t[:, :128], t[:, 128:]
    return g_re * t_re + g_im * t_im, g_im * t_re - g_re * t_im


def kernel(
    x_ref, t_ref, o_ref, ix_h, iy_h, bx_h, by_h, ky_h, kx_h,
    out_ref,
    pixels_in, box_in, wanted, ext, ext_hi, ext_lo, own, bank, mine, some, piece, boxes,
    stat_a, stats_a, stat_b, stats_b, image, corr, got,
    ix, iy, bx, by, ky, kx,
    own_sem, table_sem, halo_s, halo_r, bank_s, bank_r, some_s, some_r, box_s, box_r,
    down_s, up_s, sa_r, sb_s, sb_r, out_s, out_r,
):
    z = lax.axis_index("oy")
    a = lax.axis_index("ox")
    j = lax.axis_index("ori")
    core = lax.rem(a, 2)
    partner = a + 1 - 2 * core
    half = lax.rem(z, 2)
    beside = z + 1 - 2 * half

    def turn(v, d):
        return lax.rem(v + d, 8)

    ori_peers = [{"ori": turn(j, d)} for d in range(1, 8)]
    pair_peers = [{"ox": partner, "ori": turn(j, d)} for d in range(8)]
    ox_peers = [{"ox": turn(a, d)} for d in range(1, 8)]
    hi_peers = [{"ox": turn(a, 2 * d)} for d in range(1, 4)]
    box_peers = [{"ox": partner}, {"oy": beside}, {"oy": beside, "ox": partner}]

    barrier = pltpu.get_barrier_semaphore()

    def greet(peer):
        pl.semaphore_signal(barrier, inc=1, device_id=peer, device_id_type=MESH)

    sides = ((1, z < 7, z > 0), (-1, z > 0, z < 7))
    for dz, there, _ in sides:

        @pl.when(there)
        def _(dz=dz):
            greet({"oy": z + dz})

    for peer in ox_peers + pair_peers[1:] + ori_peers + box_peers[2:]:
        greet(peer)
    for d in range(2, 8):

        @pl.when(z + d < 8)
        def _(d=d):
            greet({"oy": z + d})

    greetings = (
        22
        + jnp.where(z > 0, 1, 0)
        + jnp.where(z < 7, 1, 0)
        + jnp.where(z > 1, z - 1, 0)
    )

    own_loads = [
        pltpu.make_async_copy(src, dst, own_sem.at[k])
        for k, (src, dst) in enumerate(((x_ref, pixels_in), (t_ref, box_in), (o_ref, wanted)))
    ]
    loads = [
        pltpu.make_async_copy(src, dst, table_sem.at[k])
        for k, (src, dst) in enumerate(
            ((ix_h, ix), (iy_h, iy), (bx_h, bx), (by_h, by), (ky_h, ky), (kx_h, kx))
        )
    ]
    for load in own_loads + loads:
        load.start()
    for load in own_loads:
        load.wait()

    own[0] = box_in[0, :, 0:128]
    own[1] = jnp.zeros((BOX, 128), BF16)
    own[1, :, 0 : BOX - 128] = box_in[0, :, 128:BOX]

    pixels = pixels_in[...]
    count = float(TILE * TILE)
    tile_mean = jnp.sum(jnp.sum(pixels, 0, keepdims=True), 1, keepdims=True) / count
    off = pixels - tile_mean
    tile_dev = jnp.sum(jnp.sum(off * off, 0, keepdims=True), 1, keepdims=True)
    row = lax.broadcasted_iota(jnp.int32, (8, 128), 0)
    stat_a[...] = jnp.where(row == 0, tile_mean, tile_dev)
    stats_a[z] = stat_a[...]

    pl.semaphore_wait(barrier, greetings)

    def copier(src, dst, s, r, peer):
        return pltpu.make_async_remote_copy(
            src_ref=src, dst_ref=dst, send_sem=s, recv_sem=r, device_id=peer, device_id_type=MESH
        )

    def send(*what):
        copy = copier(*what)
        copy.start()
        return copy

    mid_rows = pl.ds(pl.multiple_of(half * PART, 16), PART)
    bank_copies = [
        send(
            own.at[core if k < 7 else 1 - core, mid_rows],
            bank.at[k], bank_s.at[k], bank_r.at[k], peer,
        )
        for k, peer in enumerate(ori_peers + pair_peers)
    ]

    def tell(d, s):
        return copier(stat_a, stats_a.at[z], s.at[abs(d) - 1], sa_r.at[z], {"oy": z + d})

    def heard(d):
        copier(stat_a, stats_a.at[z + d], up_s.at[0], sa_r.at[z + d], {"oy": z + d}).wait_recv()

    for d in range(1, 8):

        @pl.when(z - d >= 0)
        def _(d=d):
            tell(-d, down_s).start()

    row_kind = {-1: (0, 256), 1: (TILE - HALF, 352)}
    across = [
        send(
            pixels_in.at[:, pl.ds(c_from, 128)], ext.at[pl.ds(0, TILE), pl.ds(c_to, 128)],
            halo_s.at[k], halo_r.at[k], {"ox": turn(a, da)},
        )
        for k, (da, c_from, c_to) in enumerate(((1, 128, 384), (7, 0, 256)))
    ]

    def along(k, dz, source, lanes):
        r_from, r_to = row_kind[dz]
        return copier(
            source.at[pl.ds(r_from, HALF), lanes], ext.at[pl.ds(r_to, HALF), lanes],
            halo_s.at[k], halo_r.at[k], {"oy": z + dz},
        )

    def straight(n):
        return along(2 + n, sides[n][0], pixels_in, pl.ds(0, 256))

    def corners(n):
        return along(4 + n, sides[n][0], ext, pl.ds(256, 256))

    for n in range(2):

        @pl.when(sides[n][1])
        def _(n=n):
            straight(n).start()

    totals = []
    for slot in range(2):
        local = own[core, mid_rows, :].astype(F32)
        totals.append(jnp.where(a * 8 + j == wanted[slot], 1.0, 0.0) * local)
    for k, copy in enumerate(bank_copies):
        copy.wait()
        d = k + 1 if k < 7 else k - 7
        column = a if k < 7 else partner
        entry = column * 8 + lax.rem(j + 8 - d, 8)
        arrived = bank[k].astype(F32)
        for slot in range(2):
            totals[slot] += jnp.where(entry == wanted[slot], 1.0, 0.0) * arrived
    some_copies = []
    for slot in range(2):
        mine[slot] = totals[slot].astype(BF16)
        for k, peer in enumerate(hi_peers):
            n = slot * 3 + k
            some_copies.append(send(mine.at[slot], some.at[n], some_s.at[n], some_r.at[n], peer))

    def merge(tiles, number):
        means = [t[0:1, :] for t in tiles]
        mid = sum(means) * 0.125
        dev = sum(t[1:2, :] for t in tiles) + number * sum((m - mid) * (m - mid) for m in means)
        return mid, dev

    for copy in across:
        copy.wait()
    for n in range(2):

        @pl.when(sides[n][1])
        def _(n=n):
            corners(n).start()

    for d in range(1, 8):

        @pl.when(z + d < 8)
        def _(d=d):
            heard(d)
            tell(d, up_s).start()

    for d in range(1, 8):

        @pl.when(z - d >= 0)
        def _(d=d):
            heard(-d)

    mid, dev = merge([stats_a.at[k] for k in range(8)], count)
    stat_b[...] = jnp.where(row == 0, mid, dev)
    stat_copies = [
        send(stat_b, stats_b.at[k], sb_s.at[k], sb_r.at[k], peer) for k, peer in enumerate(ox_peers)
    ]

    box_copies = []
    for slot in range(2):
        total = mine[slot].astype(F32)
        for k in range(3):
            some_copies[slot * 3 + k].wait()
            total += some[slot * 3 + k].astype(F32)
        piece[slot] = total.astype(BF16)
        boxes[slot, core, mid_rows, :] = piece[slot]
        for k, peer in enumerate(box_peers):
            n = slot * 3 + k
            box_copies.append(
                send(piece.at[slot], boxes.at[slot, core, mid_rows], box_s.at[n], box_r.at[n], peer)
            )

    for copy_of in (straight, corners):
        for n in range(2):

            @pl.when(sides[n][1])
            def _(n=n, copy_of=copy_of):
                copy_of(n).wait_send()

            @pl.when(sides[n][2])
            def _(n=n, copy_of=copy_of):
                copy_of(n).wait_recv()

    for r_at, r_size, r_ok in ((0, 256, None), (256, HALF, z < 7), (352, HALF, z > 0)):
        for c_at, c_size, c_ok in ((0, 256, None), (256, 128, a < 7), (384, 128, a > 0)):
            if r_at == 0 and c_at == 0:
                values = pixels_in[...] - tile_mean
            else:
                values = ext[r_at : r_at + r_size, c_at : c_at + c_size] - tile_mean
            for ok in (r_ok, c_ok):
                if ok is not None:
                    values = jnp.where(ok, values, 0.0)
            high, low = split(values)
            ext_hi[r_at : r_at + r_size, c_at : c_at + c_size] = high
            ext_lo[r_at : r_at + r_size, c_at : c_at + c_size] = low

    for load in loads:
        load.wait()

    for tau in range(2):
        at = slice(tau * 256, tau * 256 + 256)
        whole = jnp.concatenate([ext_hi[...], ext_lo[...], ext_hi[...]], axis=1)
        lines = mul(whole, ix[:, at])
        upper, lower = lines[:FOLD], lines[FOLD:]
        even = mul(iy[0], left_of(upper + lower))
        odd = mul(iy[1], left_of(upper - lower))
        quarter = FOLD // 2
        image[0, :, at], image[1, :, at] = both_ways(
            jnp.concatenate([even[:quarter], odd[:quarter], even[quarter:], odd[quarter:]], axis=0)
        )

    y_at = lax.broadcasted_iota(jnp.int32, (TILE, BOX), 0)
    u_at = lax.broadcasted_iota(jnp.int32, (TILE, BOX), 1)
    line = z * TILE + y_at + u_at - HALF
    row_in = jnp.where((line >= 0) & (line < 8 * TILE), 1.0, 0.0).astype(BF16)
    v_at = lax.broadcasted_iota(jnp.int32, (TILE, TILE), 0)
    x_at = lax.broadcasted_iota(jnp.int32, (TILE, TILE), 1)
    line = a * TILE + x_at + v_at - HALF
    col_in = jnp.where((line >= 0) & (line < 8 * TILE), 1.0, 0.0).astype(BF16)

    out_copies = []
    for slot in range(2):
        for k in range(3):
            box_copies[slot * 3 + k].wait()
        box = jnp.concatenate([boxes[slot, 0], boxes[slot, 1]], axis=1)

        twice = jnp.concatenate([box, box], axis=1)
        parts = []
        for tau in range(2):
            at = slice(tau * 256, tau * 256 + 256)
            t_plus, t_minus = both_ways(mul(by[...], left_of(mul(twice, bx[:, at]))))
            p_re, p_im = conj_product(image[0, :, at], t_plus)
            m_re, m_im = conj_product(image[1, :, at], t_minus)
            first = lax.broadcasted_iota(jnp.int32, (FOLD, 128), 0) == 0
            joint = jnp.concatenate(
                [
                    jnp.concatenate(
                        [p_re + jnp.where(first, 0.0, m_re), p_im + jnp.where(first, 0.0, m_im)],
                        axis=1,
                    ),
                    jnp.concatenate(
                        [jnp.where(first, m_re, m_im - p_im), jnp.where(first, m_im, p_re - m_re)],
                        axis=1,
                    ),
                ],
                axis=0,
            )
            parts.append(mul(left_of(mul(ky[...], left_of(joint)), 1), kx[tau]))
        high, low = split(mul(row_in, box))
        cover = mul(high, col_in) + mul(low, col_in)

        if slot == 0:
            for copy in stat_copies:
                copy.wait()
            mid, dev = merge([stat_b] + [stats_b.at[k] for k in range(7)], count * 8)
            scale = 1.0 / jnp.sqrt(dev[:, 0:1] / (count * 64) + 1e-06)
            rest = mid[:, 0:1] - tile_mean
        corr[slot] = parts[0] + parts[1] - rest * cover

        for d in range(1, 8):
            to = turn(j, d)
            k = slot * 7 + d - 1
            out_copies.append(
                send(
                    corr.at[slot, pl.ds(pl.multiple_of(to * BAND, BAND), BAND)],
                    got.at[k], out_s.at[k], out_r.at[k], {"ori": to},
                )
            )

    band = pl.ds(pl.multiple_of(j * BAND, BAND), BAND)
    one, two = corr[0, band, :], corr[1, band, :]
    best = jnp.maximum(one, two)
    summed = one + two
    squared = one * one + two * two
    for k, copy in enumerate(out_copies):
        copy.wait()
        value = got[k]
        best = jnp.maximum(best, value)
        summed += value
        squared += value * value
    out_ref[0] = best * scale
    out_ref[1] = summed * scale
    out_ref[2] = squared * (scale * scale)
    for d in range(1, 8):

        @pl.when(z - d >= 0)
        def _(d=d):
            tell(-d, down_s).wait_send()

        @pl.when(z + d < 8)
        def _(d=d):
            tell(d, up_s).wait_send()


def body(micrograph, projections, orientations):
    consts = tables()
    vmem = pl.BlockSpec(memory_space=pltpu.VMEM)
    hbm = pl.BlockSpec(memory_space=pl.ANY)
    dma = pltpu.SemaphoreType.DMA
    out = jax.ShapeDtypeStruct((3, BAND, TILE), F32)
    scratch = [
        pltpu.VMEM((TILE, TILE), F32),
        pltpu.VMEM((1, BOX, BOX), BF16),
        pltpu.SMEM((2,), jnp.int32),
        pltpu.VMEM((LEN, 512), F32),
        pltpu.VMEM((LEN, 512), BF16),
        pltpu.VMEM((LEN, 512), BF16),
        pltpu.VMEM((2, BOX, 128), BF16),
        pltpu.VMEM((15, PART, 128), BF16),
        pltpu.VMEM((2, PART, 128), BF16),
        pltpu.VMEM((6, PART, 128), BF16),
        pltpu.VMEM((2, PART, 128), BF16),
        pltpu.VMEM((2, 2, BOX, 128), BF16),
        pltpu.VMEM((8, 128), F32),
        pltpu.VMEM((8, 8, 128), F32),
        pltpu.VMEM((8, 128), F32),
        pltpu.VMEM((7, 8, 128), F32),
        pltpu.VMEM((2, FOLD, 512), F32),
        pltpu.VMEM((2, TILE, TILE), F32),
        pltpu.VMEM((14, BAND, TILE), F32),
    ]
    scratch += [pltpu.VMEM(c.shape, BF16) for c in consts]
    for n in (3, 6, 6, 6, 15, 15, 6, 6, 6, 6, 7, 7, 8, 7, 7, 14, 14):
        scratch.append(dma((n,)))
    stats = pl.pallas_call(
        kernel,
        out_shape=out,
        in_specs=[hbm] * 9,
        out_specs=vmem,
        scratch_shapes=scratch,
        name="match",
        compiler_params=pltpu.CompilerParams(
            collective_id=0, has_side_effects=True, vmem_limit_bytes=60 * 1024 * 1024
        ),
    )(micrograph, projections, orientations, *[jnp.asarray(c) for c in consts])
    return stats[0], stats[1] / 16.0, stats[2] / 16.0


def solution(mesh):
    in_specs = (P("oy", "ox"), P(("ox", "ori"), None, None), P("ori"))
    out_specs = (P(("oy", "ori"), "ox"), P(("oy", "ori"), "ox"), P(("oy", "ori"), "ox"))
    return jax.shard_map(body, mesh=mesh, in_specs=in_specs, out_specs=out_specs, check_vma=False)
```

```python
import functools
import math

import jax
import jax.numpy as jnp
import ml_dtypes
import numpy as np
from jax import lax
from jax.experimental import pallas as pl
from jax.experimental.pallas import tpu as pltpu
from jax.sharding import PartitionSpec as P

MESH = pl.DeviceIdType.MESH
BF16 = jnp.bfloat16
F32 = jnp.float32

TILE = 256
BOX = 192
HALF = 96
LEN = 448
FOLD = LEN // 2
ROWS = 288
PART = 80
BAND = 32
FREQS = LEN // 2 + 1
FAR_FIRST = (2, 6, 3, 5, 1, 7, 4)


def trig(rows, cols):
    turns = np.outer(rows, cols) % LEN
    phase = turns * (2.0 * math.pi / LEN)
    return np.cos(phase), np.sin(phase)


def stacked(table, axis, order):
    table = table.astype(np.float32)
    high = table.astype(ml_dtypes.bfloat16)
    low = (table - high.astype(np.float32)).astype(ml_dtypes.bfloat16)
    return np.concatenate([{"h": high, "l": low}[c] for c in order], axis)


def waves(freqs, places):
    cosine, sine = trig(freqs, places)
    if freqs[0] == 0:
        sine[0] = np.cos(math.pi * places)
    return cosine, sine


def tables():
    freq = np.arange(256)
    live = freq < FREQS

    def by_tile(re_part, im_part, axis):
        re_lo, re_hi = np.split(re_part, 2, axis)
        im_lo, im_hi = np.split(im_part, 2, axis)
        return np.concatenate([re_lo, im_lo, re_hi, im_hi], axis)

    lane = np.arange(512)
    place = np.where(lane < 352, lane, lane - 64)
    used = (lane < 352) | (lane >= 416)
    cosine, sine = trig(place, freq)
    keep = used[:, None] & live[None, :]
    image_x = stacked(by_tile(cosine * keep, -sine * keep, 1), 0, "hhl")

    near = np.arange(FOLD)
    even, odd = np.arange(0, FOLD, 2), np.arange(1, FOLD, 2)
    image_y = stacked(np.stack([np.concatenate(waves(k, near), 0) for k in (even, odd)]), 2, "hhl")

    column = np.arange(256)
    cosine, sine = trig(column - HALF, freq)
    keep = (column < BOX)[:, None] & live[None, :]
    box_x = stacked(by_tile(cosine * keep, -sine * keep, 1), 0, "hl")

    order = np.concatenate([even, odd])
    box_y = stacked(np.concatenate(waves(order, np.arange(BOX) - HALF), 0), 1, "hhl")

    pixel = np.arange(TILE)
    back_y = stacked(np.concatenate([w.T for w in waves(order, pixel)], 1), 1, "hhl")

    cosine, sine = trig(freq, pixel)
    share = np.where((freq == 0) | (freq == FREQS - 1), 1.0, 2.0) * live / (LEN * LEN)
    back_x = by_tile(cosine * share[:, None], -sine * share[:, None], 0)
    back_x = stacked(back_x.reshape(2, 256, TILE), 1, "hhl")
    return [image_x, image_y, box_x, box_y, back_y, back_x]


def split(values):
    high = values.astype(BF16)
    return high, (values - high.astype(F32)).astype(BF16)


def mul(left, right):
    return jnp.dot(left, right, preferred_element_type=F32)


def left_of(values, axis=0):
    high, low = split(values)
    return jnp.concatenate([high, low, high], axis=axis)


def both_ways(both):
    even, odd = both[:FOLD], both[FOLD:]
    first = lax.broadcasted_iota(jnp.int32, even.shape, 0) == 0
    turned = jnp.concatenate([odd[:, 128:], -odd[:, :128]], axis=1)
    plus = even + jnp.where(first, 0.0, turned)
    minus = jnp.where(first, odd, even - turned)
    return plus, minus


def conj_product(g, t):
    g_re, g_im, t_re, t_im = g[:, :128], g[:, 128:], t[:, :128], t[:, 128:]
    return g_re * t_re + g_im * t_im, g_im * t_re - g_re * t_im


def kernel(
    x_ref, t_ref, o_ref, ix_h, iy_h, bx_h, by_h, ky_h, kx_h,
    out_ref,
    pixels_in, box_in, wanted, ext, ext_hi, ext_lo, own, bank, mine, some, piece, boxes,
    stat_a, stats_a, stat_b, stats_b, image, corr, got,
    ix, iy, bx, by, ky, kx,
    own_sem, table_sem, halo_s, halo_r, bank_s, bank_r, some_s, some_r, box_s, box_r,
    down_s, up_s, sa_r, sb_s, sb_r, out_s, out_r,
):
    z = lax.axis_index("oy")
    a = lax.axis_index("ox")
    j = lax.axis_index("ori")
    core = lax.rem(a, 2)
    partner = a + 1 - 2 * core
    half = lax.rem(z, 2)
    beside = z + 1 - 2 * half

    def turn(v, d):
        return lax.rem(v + d, 8)

    ori_peers = [{"ori": turn(j, d)} for d in range(1, 8)]
    pair_peers = [{"ox": partner, "ori": turn(j, d)} for d in range(8)]
    ox_peers = [{"ox": turn(a, d)} for d in range(1, 8)]
    hi_peers = [{"ox": turn(a, 2 * d)} for d in (2, 1, 3)]
    box_peers = [{"ox": partner}, {"oy": beside}, {"oy": beside, "ox": partner}]

    barrier = pltpu.get_barrier_semaphore()

    def greet(peer):
        pl.semaphore_signal(barrier, inc=1, device_id=peer, device_id_type=MESH)

    for peer in ox_peers + pair_peers[1:] + ori_peers + box_peers[2:]:
        greet(peer)
    sides = ((1, z < 7, z > 0), (-1, z > 0, z < 7))
    for dz, there, _ in sides:

        @pl.when(there)
        def _(dz=dz):
            greet({"oy": z + dz})

    for d in range(2, 8):

        @pl.when(z + d < 8)
        def _(d=d):
            greet({"oy": z + d})

    greetings = (
        22
        + jnp.where(z > 0, 1, 0)
        + jnp.where(z < 7, 1, 0)
        + jnp.where(z > 1, z - 1, 0)
    )

    own_loads = [
        pltpu.make_async_copy(src, dst, own_sem.at[k])
        for k, (src, dst) in enumerate(((x_ref, pixels_in), (t_ref, box_in), (o_ref, wanted)))
    ]
    loads = [
        pltpu.make_async_copy(src, dst, table_sem.at[k])
        for k, (src, dst) in enumerate(
            ((ix_h, ix), (iy_h, iy), (bx_h, bx), (by_h, by), (ky_h, ky), (kx_h, kx))
        )
    ]
    for load in own_loads + loads:
        load.start()
    for load in own_loads:
        load.wait()

    own[0:BOX] = box_in[0, :, 0:128]
    tail = box_in[0, :, 128:BOX].astype(F32)
    own[BOX:ROWS] = jnp.concatenate([tail[: BOX // 2], tail[BOX // 2 :]], axis=1).astype(BF16)

    pixels = pixels_in[...]
    count = float(TILE * TILE)
    tile_mean = jnp.sum(jnp.sum(pixels, 0, keepdims=True), 1, keepdims=True) / count
    off = pixels - tile_mean
    tile_dev = jnp.sum(jnp.sum(off * off, 0, keepdims=True), 1, keepdims=True)
    row = lax.broadcasted_iota(jnp.int32, (8, 128), 0)
    stat_a[...] = jnp.where(row == 0, tile_mean, tile_dev)
    stats_a[z] = stat_a[...]

    pl.semaphore_wait(barrier, greetings)

    def copier(src, dst, s, r, peer):
        return pltpu.make_async_remote_copy(
            src_ref=src, dst_ref=dst, send_sem=s, recv_sem=r, device_id=peer, device_id_type=MESH
        )

    def send(*what):
        copy = copier(*what)
        copy.start()
        return copy

    def part_of(core):
        return pl.ds(pl.multiple_of(half * (ROWS // 2) + core * 64, 16), PART)

    bank_copies = [
        copier(
            own.at[part_of(core if k < 7 else 1 - core)],
            bank.at[k], bank_s.at[k], bank_r.at[k], peer,
        )
        for k, peer in enumerate(ori_peers + pair_peers)
    ]
    for d in FAR_FIRST:
        bank_copies[7 + d].start()
        bank_copies[d - 1].start()
    bank_copies[7].start()

    def tell(d, s):
        return copier(stat_a, stats_a.at[z], s.at[abs(d) - 1], sa_r.at[z], {"oy": z + d})

    def heard(d):
        copier(stat_a, stats_a.at[z + d], up_s.at[0], sa_r.at[z + d], {"oy": z + d}).wait_recv()

    for d in range(1, 8):

        @pl.when(z - d >= 0)
        def _(d=d):
            tell(-d, down_s).start()

    row_kind = {-1: (0, 256), 1: (TILE - HALF, 352)}
    across = [
        send(
            pixels_in.at[:, pl.ds(c_from, 128)], ext.at[pl.ds(0, TILE), pl.ds(c_to, 128)],
            halo_s.at[k], halo_r.at[k], {"ox": turn(a, da)},
        )
        for k, (da, c_from, c_to) in enumerate(((1, 128, 384), (7, 0, 256)))
    ]

    def along(k, dz, source, lanes):
        r_from, r_to = row_kind[dz]
        return copier(
            source.at[pl.ds(r_from, HALF), lanes], ext.at[pl.ds(r_to, HALF), lanes],
            halo_s.at[k], halo_r.at[k], {"oy": z + dz},
        )

    def straight(n):
        return along(2 + n, sides[n][0], pixels_in, pl.ds(0, 256))

    def corners(n):
        return along(4 + n, sides[n][0], ext, pl.ds(256, 256))

    for n in range(2):

        @pl.when(sides[n][1])
        def _(n=n):
            straight(n).start()

    totals = []
    for slot in range(2):
        local = own[part_of(core), :].astype(F32)
        totals.append(jnp.where(a * 8 + j == wanted[slot], 1.0, 0.0) * local)
    for k, copy in enumerate(bank_copies):
        copy.wait()
        d = k + 1 if k < 7 else k - 7
        column = a if k < 7 else partner
        entry = column * 8 + lax.rem(j + 8 - d, 8)
        arrived = bank[k].astype(F32)
        for slot in range(2):
            totals[slot] += jnp.where(entry == wanted[slot], 1.0, 0.0) * arrived
    some_copies = []
    for slot in range(2):
        mine[slot] = totals[slot].astype(BF16)
        for k, peer in enumerate(hi_peers):
            n = slot * 3 + k
            some_copies.append(send(mine.at[slot], some.at[n], some_s.at[n], some_r.at[n], peer))

    def merge(tiles, number):
        means = [t[0:1, :] for t in tiles]
        mid = sum(means) * 0.125
        dev = sum(t[1:2, :] for t in tiles) + number * sum((m - mid) * (m - mid) for m in means)
        return mid, dev

    for copy in across:
        copy.wait()
    for n in range(2):

        @pl.when(sides[n][1])
        def _(n=n):
            corners(n).start()

    for d in range(1, 8):

        @pl.when(z + d < 8)
        def _(d=d):
            heard(d)
            tell(d, up_s).start()

    for d in range(1, 8):

        @pl.when(z - d >= 0)
        def _(d=d):
            heard(-d)

    mid, dev = merge([stats_a.at[k] for k in range(8)], count)
    stat_b[...] = jnp.where(row == 0, mid, dev)
    stat_copies = [
        send(stat_b, stats_b.at[k], sb_s.at[k], sb_r.at[k], peer) for k, peer in enumerate(ox_peers)
    ]

    box_copies = []
    for slot in range(2):
        total = mine[slot].astype(F32)
        for k in range(3):
            some_copies[slot * 3 + k].wait()
            total += some[slot * 3 + k].astype(F32)
        piece[slot] = total.astype(BF16)
        for k, peer in enumerate(box_peers):
            n = slot * 3 + k
            box_copies.append(
                send(piece.at[slot], boxes.at[n], box_s.at[n], box_r.at[n], peer)
            )

    for copy_of in (straight, corners):
        for n in range(2):

            @pl.when(sides[n][1])
            def _(n=n, copy_of=copy_of):
                copy_of(n).wait_send()

            @pl.when(sides[n][2])
            def _(n=n, copy_of=copy_of):
                copy_of(n).wait_recv()

    for r_at, r_size, r_ok in ((0, 256, None), (256, HALF, z < 7), (352, HALF, z > 0)):
        for c_at, c_size, c_ok in ((0, 256, None), (256, 128, a < 7), (384, 128, a > 0)):
            if r_at == 0 and c_at == 0:
                values = pixels_in[...] - tile_mean
            else:
                values = ext[r_at : r_at + r_size, c_at : c_at + c_size] - tile_mean
            for ok in (r_ok, c_ok):
                if ok is not None:
                    values = jnp.where(ok, values, 0.0)
            high, low = split(values)
            ext_hi[r_at : r_at + r_size, c_at : c_at + c_size] = high
            ext_lo[r_at : r_at + r_size, c_at : c_at + c_size] = low

    for load in loads:
        load.wait()

    for tau in range(2):
        at = slice(tau * 256, tau * 256 + 256)
        whole = jnp.concatenate([ext_hi[...], ext_lo[...], ext_hi[...]], axis=1)
        lines = mul(whole, ix[:, at])
        upper, lower = lines[:FOLD], lines[FOLD:]
        even = mul(iy[0], left_of(upper + lower))
        odd = mul(iy[1], left_of(upper - lower))
        quarter = FOLD // 2
        image[0, :, at], image[1, :, at] = both_ways(
            jnp.concatenate([even[:quarter], odd[:quarter], even[quarter:], odd[quarter:]], axis=0)
        )

    y_at = lax.broadcasted_iota(jnp.int32, (TILE, BOX), 0)
    u_at = lax.broadcasted_iota(jnp.int32, (TILE, BOX), 1)
    line = z * TILE + y_at + u_at - HALF
    row_in = jnp.where((line >= 0) & (line < 8 * TILE), 1.0, 0.0).astype(BF16)
    v_at = lax.broadcasted_iota(jnp.int32, (TILE, TILE), 0)
    x_at = lax.broadcasted_iota(jnp.int32, (TILE, TILE), 1)
    line = a * TILE + x_at + v_at - HALF
    col_in = jnp.where((line >= 0) & (line < 8 * TILE) & (v_at < BOX), 1.0, 0.0).astype(BF16)

    out_copies = []
    for slot in range(2):
        for k in range(3):
            box_copies[slot * 3 + k].wait()
        here, there = (
            [first.astype(F32), second.astype(F32)]
            for first, second in (
                (piece[slot], boxes[slot * 3]),
                (boxes[slot * 3 + 1], boxes[slot * 3 + 2]),
            )
        )
        here, there = (
            jnp.concatenate(
                [jnp.where(core == 0, p, q), jnp.where(core == 0, q, p)[2 * PART - ROWS // 2 :]],
                axis=0,
            )
            for p, q in (here, there)
        )
        flat = jnp.concatenate(
            [jnp.where(half == 0, here, there), jnp.where(half == 0, there, here)], axis=0
        )
        tail = flat[BOX:]
        tail = jnp.concatenate([tail, pltpu.roll(tail, 64, 1)], axis=0)
        box = jnp.concatenate([flat[:BOX].astype(BF16), tail.astype(BF16)], axis=1)

        twice = jnp.concatenate([box, box], axis=1)
        parts = []
        for tau in range(2):
            at = slice(tau * 256, tau * 256 + 256)
            t_plus, t_minus = both_ways(mul(by[...], left_of(mul(twice, bx[:, at]))))
            p_re, p_im = conj_product(image[0, :, at], t_plus)
            m_re, m_im = conj_product(image[1, :, at], t_minus)
            first = lax.broadcasted_iota(jnp.int32, (FOLD, 128), 0) == 0
            joint = jnp.concatenate(
                [
                    jnp.concatenate(
                        [p_re + jnp.where(first, 0.0, m_re), p_im + jnp.where(first, 0.0, m_im)],
                        axis=1,
                    ),
                    jnp.concatenate(
                        [jnp.where(first, m_re, m_im - p_im), jnp.where(first, m_im, p_re - m_re)],
                        axis=1,
                    ),
                ],
                axis=0,
            )
            parts.append(mul(left_of(mul(ky[...], left_of(joint)), 1), kx[tau]))
        high, low = split(mul(row_in, box))
        cover = mul(high, col_in) + mul(low, col_in)

        if slot == 0:
            for copy in stat_copies:
                copy.wait()
            mid, dev = merge([stat_b] + [stats_b.at[k] for k in range(7)], count * 8)
            scale = 1.0 / jnp.sqrt(dev[:, 0:1] / (count * 64) + 1e-06)
            rest = mid[:, 0:1] - tile_mean
        corr[slot] = parts[0] + parts[1] - rest * cover

        for d in FAR_FIRST:
            to = turn(j, d)
            k = slot * 7 + d - 1
            out_copies.append(
                send(
                    corr.at[slot, pl.ds(pl.multiple_of(to * BAND, BAND), BAND)],
                    got.at[k], out_s.at[k], out_r.at[k], {"ori": to},
                )
            )

    band = pl.ds(pl.multiple_of(j * BAND, BAND), BAND)
    one, two = corr[0, band, :], corr[1, band, :]
    best = jnp.maximum(one, two)
    summed = one + two
    squared = one * one + two * two
    for copy in out_copies:
        copy.wait()
    for k in range(14):
        value = got[k]
        best = jnp.maximum(best, value)
        summed += value
        squared += value * value
    out_ref[0] = best * scale
    out_ref[1] = summed * scale
    out_ref[2] = squared * (scale * scale)
    for d in range(1, 8):

        @pl.when(z - d >= 0)
        def _(d=d):
            tell(-d, down_s).wait_send()

        @pl.when(z + d < 8)
        def _(d=d):
            tell(d, up_s).wait_send()


def body(micrograph, projections, orientations):
    consts = tables()
    vmem = pl.BlockSpec(memory_space=pltpu.VMEM)
    hbm = pl.BlockSpec(memory_space=pl.ANY)
    dma = pltpu.SemaphoreType.DMA
    out = jax.ShapeDtypeStruct((3, BAND, TILE), F32)
    scratch = [
        pltpu.VMEM((TILE, TILE), F32),
        pltpu.VMEM((1, BOX, BOX), BF16),
        pltpu.SMEM((2,), jnp.int32),
        pltpu.VMEM((LEN, 512), F32),
        pltpu.VMEM((LEN, 512), BF16),
        pltpu.VMEM((LEN, 512), BF16),
        pltpu.VMEM((ROWS, 128), BF16),
        pltpu.VMEM((15, PART, 128), BF16),
        pltpu.VMEM((2, PART, 128), BF16),
        pltpu.VMEM((6, PART, 128), BF16),
        pltpu.VMEM((2, PART, 128), BF16),
        pltpu.VMEM((6, PART, 128), BF16),
        pltpu.VMEM((8, 128), F32),
        pltpu.VMEM((8, 8, 128), F32),
        pltpu.VMEM((8, 128), F32),
        pltpu.VMEM((7, 8, 128), F32),
        pltpu.VMEM((2, FOLD, 512), F32),
        pltpu.VMEM((2, TILE, TILE), F32),
        pltpu.VMEM((14, BAND, TILE), F32),
    ]
    scratch += [pltpu.VMEM(c.shape, BF16) for c in consts]
    for n in (3, 6, 6, 6, 15, 15, 6, 6, 6, 6, 7, 7, 8, 7, 7, 14, 14):
        scratch.append(dma((n,)))
    stats = pl.pallas_call(
        kernel,
        out_shape=out,
        in_specs=[hbm] * 9,
        out_specs=vmem,
        scratch_shapes=scratch,
        name="match",
        compiler_params=pltpu.CompilerParams(
            collective_id=0, has_side_effects=True, vmem_limit_bytes=60 * 1024 * 1024
        ),
    )(micrograph, projections, orientations, *[jnp.asarray(c) for c in consts])
    return stats[0], stats[1] / 16.0, stats[2] / 16.0


def solution(mesh):
    in_specs = (P("oy", "ox"), P(("ox", "ori"), None, None), P("ori"))
    out_specs = (P(("oy", "ori"), "ox"), P(("oy", "ori"), "ox"), P(("oy", "ori"), "ox"))
    return jax.shard_map(body, mesh=mesh, in_specs=in_specs, out_specs=out_specs, check_vma=False)
```

```python
import functools
import math

import jax
import jax.numpy as jnp
import ml_dtypes
import numpy as np
from jax import lax
from jax.experimental import pallas as pl
from jax.experimental.pallas import tpu as pltpu
from jax.sharding import PartitionSpec as P

MESH = pl.DeviceIdType.MESH
BF16 = jnp.bfloat16
F32 = jnp.float32

TILE = 256
BOX = 192
HALF = 96
LEN = 448
FOLD = LEN // 2
ROWS = 288
PART = 80
BAND = 32
FREQS = LEN // 2 + 1
FAR_FIRST = (2, 6, 3, 5, 1, 7, 4)


def trig(rows, cols):
    turns = np.outer(rows, cols) % LEN
    phase = turns * (2.0 * math.pi / LEN)
    return np.cos(phase), np.sin(phase)


def stacked(table, axis, order):
    table = table.astype(np.float32)
    high = table.astype(ml_dtypes.bfloat16)
    low = (table - high.astype(np.float32)).astype(ml_dtypes.bfloat16)
    return np.concatenate([{"h": high, "l": low}[c] for c in order], axis)


def waves(freqs, places):
    cosine, sine = trig(freqs, places)
    if freqs[0] == 0:
        sine[0] = np.cos(math.pi * places)
    return cosine, sine


def tables():
    freq = np.arange(256)
    live = freq < FREQS

    def by_tile(re_part, im_part, axis):
        re_lo, re_hi = np.split(re_part, 2, axis)
        im_lo, im_hi = np.split(im_part, 2, axis)
        return np.concatenate([re_lo, im_lo, re_hi, im_hi], axis)

    lane = np.arange(512)
    place = np.where(lane < 352, lane, lane - 64)
    used = (lane < 352) | (lane >= 416)
    cosine, sine = trig(place, freq)
    keep = used[:, None] & live[None, :]
    image_x = stacked(by_tile(cosine * keep, -sine * keep, 1), 0, "hhl")

    near = np.arange(FOLD)
    even, odd = np.arange(0, FOLD, 2), np.arange(1, FOLD, 2)
    image_y = stacked(np.stack([np.concatenate(waves(k, near), 0) for k in (even, odd)]), 2, "hhl")

    column = np.arange(256)
    cosine, sine = trig(column - HALF, freq)
    keep = (column < BOX)[:, None] & live[None, :]
    box_x = stacked(by_tile(cosine * keep, -sine * keep, 1), 0, "hl")

    order = np.concatenate([even, odd])
    box_y = stacked(np.concatenate(waves(order, np.arange(BOX) - HALF), 0), 1, "hhl")

    pixel = np.arange(TILE)
    back_y = stacked(np.concatenate([w.T for w in waves(order, pixel)], 1), 1, "hhl")

    cosine, sine = trig(freq, pixel)
    share = np.where((freq == 0) | (freq == FREQS - 1), 1.0, 2.0) * live / (LEN * LEN)
    back_x = by_tile(cosine * share[:, None], -sine * share[:, None], 0)
    back_x = stacked(back_x, 0, "hhl")
    return [image_x, image_y, box_x, box_y, back_y, back_x]


def split(values):
    high = values.astype(BF16)
    return high, (values - high.astype(F32)).astype(BF16)


def mul(left, right):
    return jnp.dot(left, right, preferred_element_type=F32)


def left_of(values, axis=0):
    high, low = split(values)
    return jnp.concatenate([high, low, high], axis=axis)


def both_ways(both):
    even, odd = both[:FOLD], both[FOLD:]
    first = lax.broadcasted_iota(jnp.int32, even.shape, 0) == 0
    turned = jnp.concatenate([odd[:, 128:], -odd[:, :128]], axis=1)
    plus = even + jnp.where(first, 0.0, turned)
    minus = jnp.where(first, odd, even - turned)
    return plus, minus


def conj_product(g, t):
    g_re, g_im, t_re, t_im = g[:, :128], g[:, 128:], t[:, :128], t[:, 128:]
    return g_re * t_re + g_im * t_im, g_im * t_re - g_re * t_im


def kernel(
    x_ref, t_ref, o_ref, ix_h, iy_h, bx_h, by_h, ky_h, kx_h,
    out_ref,
    pixels_in, box_in, wanted, ext, ext_hi, ext_lo, own, bank, mine, some, piece, boxes,
    stat_a, stats_a, stat_b, stats_b, image, corr, got,
    ix, iy, bx, by, ky, kx,
    own_sem, table_sem, halo_s, halo_r, bank_s, bank_r, some_s, some_r, box_s, box_r,
    down_s, up_s, sa_r, sb_s, sb_r, out_s, out_r,
):
    z = lax.axis_index("oy")
    a = lax.axis_index("ox")
    j = lax.axis_index("ori")
    core = lax.rem(a, 2)
    partner = a + 1 - 2 * core
    half = lax.rem(z, 2)
    beside = z + 1 - 2 * half

    def turn(v, d):
        return lax.rem(v + d, 8)

    ori_peers = [{"ori": turn(j, d)} for d in range(1, 8)]
    pair_peers = [{"ox": partner, "ori": turn(j, d)} for d in range(8)]
    ox_peers = [{"ox": turn(a, d)} for d in range(1, 8)]
    hi_peers = [{"ox": turn(a, 2 * d)} for d in (2, 1, 3)]
    box_peers = [{"ox": partner}, {"oy": beside}, {"oy": beside, "ox": partner}]

    own_loads = [
        pltpu.make_async_copy(src, dst, own_sem.at[k])
        for k, (src, dst) in enumerate(((x_ref, pixels_in), (t_ref, box_in), (o_ref, wanted)))
    ]
    for load in own_loads:
        load.start()

    barrier = pltpu.get_barrier_semaphore()

    def greet(peer):
        pl.semaphore_signal(barrier, inc=1, device_id=peer, device_id_type=MESH)

    for peer in ox_peers + pair_peers[1:] + ori_peers + box_peers[2:]:
        greet(peer)
    sides = ((1, z < 7, z > 0), (-1, z > 0, z < 7))
    for dz, there, _ in sides:

        @pl.when(there)
        def _(dz=dz):
            greet({"oy": z + dz})

    for d in range(2, 8):

        @pl.when(z + d < 8)
        def _(d=d):
            greet({"oy": z + d})

    greetings = (
        22
        + jnp.where(z > 0, 1, 0)
        + jnp.where(z < 7, 1, 0)
        + jnp.where(z > 1, z - 1, 0)
    )

    for load in own_loads:
        load.wait()

    own[0:BOX] = box_in[0, :, 0:128]
    tail = box_in[0, :, 128:BOX].astype(F32)
    own[BOX:ROWS] = jnp.concatenate([tail[: BOX // 2], tail[BOX // 2 :]], axis=1).astype(BF16)

    pl.semaphore_wait(barrier, greetings)

    def copier(src, dst, s, r, peer):
        return pltpu.make_async_remote_copy(
            src_ref=src, dst_ref=dst, send_sem=s, recv_sem=r, device_id=peer, device_id_type=MESH
        )

    def send(*what):
        copy = copier(*what)
        copy.start()
        return copy

    def part_of(core):
        return pl.ds(pl.multiple_of(half * (ROWS // 2) + core * 64, 16), PART)

    bank_copies = [
        copier(
            own.at[part_of(core if k < 7 else 1 - core)],
            bank.at[k], bank_s.at[k], bank_r.at[k], peer,
        )
        for k, peer in enumerate(ori_peers + pair_peers)
    ]
    for d in FAR_FIRST:
        bank_copies[7 + d].start()
        bank_copies[d - 1].start()
    bank_copies[7].start()

    row_kind = {-1: (0, 256), 1: (TILE - HALF, 352)}
    across = [
        send(
            pixels_in.at[:, pl.ds(c_from, 128)], ext.at[pl.ds(0, TILE), pl.ds(c_to, 128)],
            halo_s.at[k], halo_r.at[k], {"ox": turn(a, da)},
        )
        for k, (da, c_from, c_to) in enumerate(((1, 128, 384), (7, 0, 256)))
    ]

    def along(k, dz, source, lanes):
        r_from, r_to = row_kind[dz]
        return copier(
            source.at[pl.ds(r_from, HALF), lanes], ext.at[pl.ds(r_to, HALF), lanes],
            halo_s.at[k], halo_r.at[k], {"oy": z + dz},
        )

    def straight(n):
        return along(2 + n, sides[n][0], pixels_in, pl.ds(0, 256))

    def corners(n):
        return along(4 + n, sides[n][0], ext, pl.ds(256, 256))

    for n in range(2):

        @pl.when(sides[n][1])
        def _(n=n):
            straight(n).start()

    pixels = pixels_in[...]
    count = float(TILE * TILE)
    tile_mean = jnp.sum(jnp.sum(pixels, 0, keepdims=True), 1, keepdims=True) / count
    off = pixels - tile_mean
    tile_dev = jnp.sum(jnp.sum(off * off, 0, keepdims=True), 1, keepdims=True)
    row = lax.broadcasted_iota(jnp.int32, (8, 128), 0)
    stat_a[...] = jnp.where(row == 0, tile_mean, tile_dev)
    stats_a[z] = stat_a[...]

    def tell(d, s):
        return copier(stat_a, stats_a.at[z], s.at[abs(d) - 1], sa_r.at[z], {"oy": z + d})

    def heard(d):
        copier(stat_a, stats_a.at[z + d], up_s.at[0], sa_r.at[z + d], {"oy": z + d}).wait_recv()

    for d in range(1, 8):

        @pl.when(z - d >= 0)
        def _(d=d):
            tell(-d, down_s).start()

    loads = [
        pltpu.make_async_copy(src, dst, table_sem.at[k])
        for k, (src, dst) in enumerate(
            ((ix_h, ix), (iy_h, iy), (bx_h, bx), (by_h, by), (ky_h, ky), (kx_h, kx))
        )
    ]
    for load in loads:
        load.start()

    totals = []
    for slot in range(2):
        local = own[part_of(core), :].astype(F32)
        totals.append(jnp.where(a * 8 + j == wanted[slot], 1.0, 0.0) * local)
    for k, copy in enumerate(bank_copies):
        copy.wait()
        d = k + 1 if k < 7 else k - 7
        column = a if k < 7 else partner
        entry = column * 8 + lax.rem(j + 8 - d, 8)
        arrived = bank[k].astype(F32)
        for slot in range(2):
            totals[slot] += jnp.where(entry == wanted[slot], 1.0, 0.0) * arrived
    some_copies = []
    for slot in range(2):
        mine[slot] = totals[slot].astype(BF16)
        for k, peer in enumerate(hi_peers):
            n = slot * 3 + k
            some_copies.append(send(mine.at[slot], some.at[n], some_s.at[n], some_r.at[n], peer))

    def merge(tiles, number):
        means = [t[0:1, :] for t in tiles]
        mid = sum(means) * 0.125
        dev = sum(t[1:2, :] for t in tiles) + number * sum((m - mid) * (m - mid) for m in means)
        return mid, dev

    for copy in across:
        copy.wait()
    for n in range(2):

        @pl.when(sides[n][1])
        def _(n=n):
            corners(n).start()

    for d in range(1, 8):

        @pl.when(z + d < 8)
        def _(d=d):
            heard(d)
            tell(d, up_s).start()

    for d in range(1, 8):

        @pl.when(z - d >= 0)
        def _(d=d):
            heard(-d)

    mid, dev = merge([stats_a.at[k] for k in range(8)], count)
    stat_b[...] = jnp.where(row == 0, mid, dev)
    stat_copies = [
        send(stat_b, stats_b.at[k], sb_s.at[k], sb_r.at[k], peer) for k, peer in enumerate(ox_peers)
    ]

    box_copies = []
    for slot in range(2):
        total = mine[slot].astype(F32)
        for k in range(3):
            some_copies[slot * 3 + k].wait()
            total += some[slot * 3 + k].astype(F32)
        piece[slot] = total.astype(BF16)
        for k, peer in enumerate(box_peers):
            n = slot * 3 + k
            box_copies.append(
                copier(piece.at[slot], boxes.at[n], box_s.at[n], box_r.at[n], peer)
            )
        for k in (2, 1, 0):
            box_copies[slot * 3 + k].start()

    for copy_of in (straight, corners):
        for n in range(2):

            @pl.when(sides[n][1])
            def _(n=n, copy_of=copy_of):
                copy_of(n).wait_send()

            @pl.when(sides[n][2])
            def _(n=n, copy_of=copy_of):
                copy_of(n).wait_recv()

    for r_at, r_size, r_ok in ((0, 256, None), (256, HALF, z < 7), (352, HALF, z > 0)):
        for c_at, c_size, c_ok in ((0, 256, None), (256, 128, a < 7), (384, 128, a > 0)):
            if r_at == 0 and c_at == 0:
                values = pixels_in[...] - tile_mean
            else:
                values = ext[r_at : r_at + r_size, c_at : c_at + c_size] - tile_mean
            for ok in (r_ok, c_ok):
                if ok is not None:
                    values = jnp.where(ok, values, 0.0)
            high, low = split(values)
            ext_hi[r_at : r_at + r_size, c_at : c_at + c_size] = high
            ext_lo[r_at : r_at + r_size, c_at : c_at + c_size] = low

    for load in loads:
        load.wait()

    whole = jnp.concatenate([ext_hi[...], ext_lo[...], ext_hi[...]], axis=1)
    lines = mul(whole, ix[...])
    upper, lower = lines[:FOLD], lines[FOLD:]
    even = mul(iy[0], left_of(upper + lower))
    odd = mul(iy[1], left_of(upper - lower))
    quarter = FOLD // 2
    both = jnp.concatenate([even[:quarter], odd[:quarter], even[quarter:], odd[quarter:]], axis=0)
    for tau in range(2):
        at = slice(tau * 256, tau * 256 + 256)
        image[0, :, at], image[1, :, at] = both_ways(both[:, at])

    y_at = lax.broadcasted_iota(jnp.int32, (TILE, BOX), 0)
    u_at = lax.broadcasted_iota(jnp.int32, (TILE, BOX), 1)
    line = z * TILE + y_at + u_at - HALF
    row_in = jnp.where((line >= 0) & (line < 8 * TILE), 1.0, 0.0).astype(BF16)
    v_at = lax.broadcasted_iota(jnp.int32, (TILE, TILE), 0)
    x_at = lax.broadcasted_iota(jnp.int32, (TILE, TILE), 1)
    line = a * TILE + x_at + v_at - HALF
    col_in = jnp.where((line >= 0) & (line < 8 * TILE) & (v_at < BOX), 1.0, 0.0).astype(BF16)

    out_copies = []
    for slot in range(2):
        for k in range(3):
            box_copies[slot * 3 + k].wait()
        here, there = (
            [first.astype(F32), second.astype(F32)]
            for first, second in (
                (piece[slot], boxes[slot * 3]),
                (boxes[slot * 3 + 1], boxes[slot * 3 + 2]),
            )
        )
        here, there = (
            jnp.concatenate(
                [jnp.where(core == 0, p, q), jnp.where(core == 0, q, p)[2 * PART - ROWS // 2 :]],
                axis=0,
            )
            for p, q in (here, there)
        )
        flat = jnp.concatenate(
            [jnp.where(half == 0, here, there), jnp.where(half == 0, there, here)], axis=0
        )
        tail = flat[BOX:]
        tail = jnp.concatenate([tail, pltpu.roll(tail, 64, 1)], axis=0)
        box = jnp.concatenate([flat[:BOX].astype(BF16), tail.astype(BF16)], axis=1)

        twice = jnp.concatenate([box, box], axis=1)
        wave = mul(by[...], left_of(mul(twice, bx[...])))
        first = lax.broadcasted_iota(jnp.int32, (FOLD, 128), 0) == 0
        joints = []
        for tau in range(2):
            at = slice(tau * 256, tau * 256 + 256)
            t_plus, t_minus = both_ways(wave[:, at])
            p_re, p_im = conj_product(image[0, :, at], t_plus)
            m_re, m_im = conj_product(image[1, :, at], t_minus)
            joint = jnp.concatenate(
                [
                    jnp.concatenate(
                        [p_re + jnp.where(first, 0.0, m_re), p_im + jnp.where(first, 0.0, m_im)],
                        axis=1,
                    ),
                    jnp.concatenate(
                        [jnp.where(first, m_re, m_im - p_im), jnp.where(first, m_im, p_re - m_re)],
                        axis=1,
                    ),
                ],
                axis=0,
            )
            joints.append(joint)
        lines = mul(ky[...], left_of(jnp.concatenate(joints, axis=1)))
        found = mul(left_of(lines, 1), kx[...])
        high, low = split(mul(row_in, box))
        cover = mul(high, col_in) + mul(low, col_in)

        if slot == 0:
            for copy in stat_copies:
                copy.wait()
            mid, dev = merge([stat_b] + [stats_b.at[k] for k in range(7)], count * 8)
            scale = 1.0 / jnp.sqrt(dev[:, 0:1] / (count * 64) + 1e-06)
            rest = mid[:, 0:1] - tile_mean
        corr[slot] = found - rest * cover

        for d in FAR_FIRST:
            to = turn(j, d)
            k = slot * 7 + d - 1
            out_copies.append(
                send(
                    corr.at[slot, pl.ds(pl.multiple_of(to * BAND, BAND), BAND)],
                    got.at[k], out_s.at[k], out_r.at[k], {"ori": to},
                )
            )

    band = pl.ds(pl.multiple_of(j * BAND, BAND), BAND)
    one, two = corr[0, band, :], corr[1, band, :]
    best = jnp.maximum(one, two)
    summed = one + two
    squared = one * one + two * two
    for copy in out_copies:
        copy.wait()
    for k in range(14):
        value = got[k]
        best = jnp.maximum(best, value)
        summed += value
        squared += value * value
    out_ref[0] = best * scale
    out_ref[1] = summed * scale
    out_ref[2] = squared * (scale * scale)
    for d in range(1, 8):

        @pl.when(z - d >= 0)
        def _(d=d):
            tell(-d, down_s).wait_send()

        @pl.when(z + d < 8)
        def _(d=d):
            tell(d, up_s).wait_send()


def body(micrograph, projections, orientations):
    consts = tables()
    vmem = pl.BlockSpec(memory_space=pltpu.VMEM)
    hbm = pl.BlockSpec(memory_space=pl.ANY)
    dma = pltpu.SemaphoreType.DMA
    out = jax.ShapeDtypeStruct((3, BAND, TILE), F32)
    scratch = [
        pltpu.VMEM((TILE, TILE), F32),
        pltpu.VMEM((1, BOX, BOX), BF16),
        pltpu.SMEM((2,), jnp.int32),
        pltpu.VMEM((LEN, 512), F32),
        pltpu.VMEM((LEN, 512), BF16),
        pltpu.VMEM((LEN, 512), BF16),
        pltpu.VMEM((ROWS, 128), BF16),
        pltpu.VMEM((15, PART, 128), BF16),
        pltpu.VMEM((2, PART, 128), BF16),
        pltpu.VMEM((6, PART, 128), BF16),
        pltpu.VMEM((2, PART, 128), BF16),
        pltpu.VMEM((6, PART, 128), BF16),
        pltpu.VMEM((8, 128), F32),
        pltpu.VMEM((8, 8, 128), F32),
        pltpu.VMEM((8, 128), F32),
        pltpu.VMEM((7, 8, 128), F32),
        pltpu.VMEM((2, FOLD, 512), F32),
        pltpu.VMEM((2, TILE, TILE), F32),
        pltpu.VMEM((14, BAND, TILE), F32),
    ]
    scratch += [pltpu.VMEM(c.shape, BF16) for c in consts]
    for n in (3, 6, 6, 6, 15, 15, 6, 6, 6, 6, 7, 7, 8, 7, 7, 14, 14):
        scratch.append(dma((n,)))
    stats = pl.pallas_call(
        kernel,
        out_shape=out,
        in_specs=[hbm] * 9,
        out_specs=vmem,
        scratch_shapes=scratch,
        name="match",
        compiler_params=pltpu.CompilerParams(
            collective_id=0, has_side_effects=True, vmem_limit_bytes=60 * 1024 * 1024
        ),
    )(micrograph, projections, orientations, *[jnp.asarray(c) for c in consts])
    return stats[0], stats[1] / 16.0, stats[2] / 16.0


def solution(mesh):
    in_specs = (P("oy", "ox"), P(("ox", "ori"), None, None), P("ori"))
    out_specs = (P(("oy", "ori"), "ox"), P(("oy", "ori"), "ox"), P(("oy", "ori"), "ox"))
    return jax.shard_map(body, mesh=mesh, in_specs=in_specs, out_specs=out_specs, check_vma=False)
```

```python
import functools
import math

import jax
import jax.numpy as jnp
import ml_dtypes
import numpy as np
from jax import lax
from jax.experimental import pallas as pl
from jax.experimental.pallas import tpu as pltpu
from jax.sharding import PartitionSpec as P

MESH = pl.DeviceIdType.MESH
BF16 = jnp.bfloat16
F32 = jnp.float32

TILE = 256
BOX = 192
HALF = 96
LEN = 448
FOLD = LEN // 2
ROWS = 288
PART = 80
BAND = 32
FREQS = LEN // 2 + 1
FAR_FIRST = (2, 6, 3, 5, 1, 7, 4)


def trig(rows, cols):
    turns = np.outer(rows, cols) % LEN
    phase = turns * (2.0 * math.pi / LEN)
    return np.cos(phase), np.sin(phase)


def stacked(table, axis, order):
    table = table.astype(np.float32)
    high = table.astype(ml_dtypes.bfloat16)
    low = (table - high.astype(np.float32)).astype(ml_dtypes.bfloat16)
    return np.concatenate([{"h": high, "l": low}[c] for c in order], axis)


def waves(freqs, places):
    cosine, sine = trig(freqs, places)
    if freqs[0] == 0:
        sine[0] = np.cos(math.pi * places)
    return cosine, sine


def tables():
    freq = np.arange(256)
    live = freq < FREQS

    def by_tile(re_part, im_part, axis):
        re_lo, re_hi = np.split(re_part, 2, axis)
        im_lo, im_hi = np.split(im_part, 2, axis)
        return np.concatenate([re_lo, im_lo, re_hi, im_hi], axis)

    lane = np.arange(512)
    place = np.where(lane < 352, lane, lane - 64)
    used = (lane < 352) | (lane >= 416)
    cosine, sine = trig(place, freq)
    keep = used[:, None] & live[None, :]
    image_x = stacked(by_tile(cosine * keep, -sine * keep, 1), 0, "hhl")

    near = np.arange(FOLD)
    even, odd = np.arange(0, FOLD, 2), np.arange(1, FOLD, 2)
    image_y = stacked(np.stack([np.concatenate(waves(k, near), 0) for k in (even, odd)]), 2, "hhl")

    column = np.arange(256)
    cosine, sine = trig(column - HALF, freq)
    keep = (column < BOX)[:, None] & live[None, :]
    box_x = stacked(by_tile(cosine * keep, -sine * keep, 1), 0, "hl")

    order = np.concatenate([even, odd])
    box_y = stacked(np.concatenate(waves(order, np.arange(BOX) - HALF), 0), 1, "hhl")

    pixel = np.arange(TILE)
    back_y = stacked(np.concatenate([w.T for w in waves(order, pixel)], 1), 1, "hhl")

    cosine, sine = trig(freq, pixel)
    share = np.where((freq == 0) | (freq == FREQS - 1), 1.0, 2.0) * live / (LEN * LEN)
    back_x = by_tile(cosine * share[:, None], -sine * share[:, None], 0)
    back_x = stacked(back_x, 0, "hhl")
    return [image_x, image_y, box_x, box_y, back_y, back_x]


def split(values):
    high = values.astype(BF16)
    return high, (values - high.astype(F32)).astype(BF16)


def mul(left, right):
    return jnp.dot(left, right, preferred_element_type=F32)


def left_of(values, axis=0):
    high, low = split(values)
    return jnp.concatenate([high, low, high], axis=axis)


def both_ways(both):
    even, odd = both[:FOLD], both[FOLD:]
    first = lax.broadcasted_iota(jnp.int32, even.shape, 0) == 0
    turned = jnp.concatenate([odd[:, 128:], -odd[:, :128]], axis=1)
    plus = even + jnp.where(first, 0.0, turned)
    minus = jnp.where(first, odd, even - turned)
    return plus, minus


def conj_product(g, t):
    g_re, g_im, t_re, t_im = g[:, :128], g[:, 128:], t[:, :128], t[:, 128:]
    return g_re * t_re + g_im * t_im, g_im * t_re - g_re * t_im


def kernel(
    x_ref, t_ref, o_ref, ix_h, iy_h, bx_h, by_h, ky_h, kx_h,
    out_ref,
    pixels_in, box_in, wanted, ext, ext_hi, ext_lo, own, bank, mine, some, piece, boxes,
    stat_a, stats_a, stat_b, stats_b, image, corr, got,
    ix, iy, bx, by, ky, kx,
    own_sem, table_sem, halo_s, halo_r, bank_s, bank_r, some_s, some_r, box_s, box_r,
    down_s, up_s, sa_r, sb_s, sb_r, out_s, out_r,
):
    z = lax.axis_index("oy")
    a = lax.axis_index("ox")
    j = lax.axis_index("ori")
    core = lax.rem(a, 2)
    partner = a + 1 - 2 * core
    half = lax.rem(z, 2)
    beside = z + 1 - 2 * half

    def turn(v, d):
        return lax.rem(v + d, 8)

    ori_peers = [{"ori": turn(j, d)} for d in range(1, 8)]
    pair_peers = [{"ox": partner, "ori": turn(j, d)} for d in range(8)]
    ox_peers = [{"ox": turn(a, d)} for d in range(1, 8)]
    hi_peers = [{"ox": turn(a, 2 * d)} for d in (2, 1, 3)]
    box_peers = [{"ox": partner}, {"oy": beside}, {"oy": beside, "ox": partner}]

    own_loads = [
        pltpu.make_async_copy(src, dst, own_sem.at[k])
        for k, (src, dst) in enumerate(((x_ref, pixels_in), (t_ref, box_in), (o_ref, wanted)))
    ]
    for load in own_loads:
        load.start()

    barrier = pltpu.get_barrier_semaphore()

    def greet(peer):
        pl.semaphore_signal(barrier, inc=1, device_id=peer, device_id_type=MESH)

    for peer in ox_peers + pair_peers[1:] + ori_peers + box_peers[2:]:
        greet(peer)
    sides = ((1, z < 7, z > 0), (-1, z > 0, z < 7))
    for dz, there, _ in sides:

        @pl.when(there)
        def _(dz=dz):
            greet({"oy": z + dz})

    for d in range(2, 8):

        @pl.when(z + d < 8)
        def _(d=d):
            greet({"oy": z + d})

    greetings = (
        22
        + jnp.where(z > 0, 1, 0)
        + jnp.where(z < 7, 1, 0)
        + jnp.where(z > 1, z - 1, 0)
    )

    for load in own_loads:
        load.wait()

    own[0:BOX] = box_in[0, :, 0:128]
    tail = box_in[0, :, 128:BOX].astype(F32)
    own[BOX:ROWS] = jnp.concatenate([tail[: BOX // 2], tail[BOX // 2 :]], axis=1).astype(BF16)

    pl.semaphore_wait(barrier, greetings)

    def copier(src, dst, s, r, peer):
        return pltpu.make_async_remote_copy(
            src_ref=src, dst_ref=dst, send_sem=s, recv_sem=r, device_id=peer, device_id_type=MESH
        )

    def send(*what):
        copy = copier(*what)
        copy.start()
        return copy

    def part_of(core):
        return pl.ds(pl.multiple_of(half * (ROWS // 2) + core * 64, 16), PART)

    bank_copies = [
        copier(
            own.at[part_of(core if k < 7 else 1 - core)],
            bank.at[k], bank_s.at[k], bank_r.at[k], peer,
        )
        for k, peer in enumerate(ori_peers + pair_peers)
    ]
    for d in FAR_FIRST:
        bank_copies[7 + d].start()
        bank_copies[d - 1].start()
    bank_copies[7].start()

    row_kind = {-1: (0, 256), 1: (TILE - HALF, 352)}
    across = [
        send(
            pixels_in.at[:, pl.ds(c_from, 128)], ext.at[pl.ds(0, TILE), pl.ds(c_to, 128)],
            halo_s.at[k], halo_r.at[k], {"ox": turn(a, da)},
        )
        for k, (da, c_from, c_to) in enumerate(((1, 128, 384), (7, 0, 256)))
    ]

    def along(k, dz, source, lanes):
        r_from, r_to = row_kind[dz]
        return copier(
            source.at[pl.ds(r_from, HALF), lanes], ext.at[pl.ds(r_to, HALF), lanes],
            halo_s.at[k], halo_r.at[k], {"oy": z + dz},
        )

    def straight(n):
        return along(2 + n, sides[n][0], pixels_in, pl.ds(0, 256))

    def corners(n):
        return along(4 + n, sides[n][0], ext, pl.ds(256, 256))

    for n in range(2):

        @pl.when(sides[n][1])
        def _(n=n):
            straight(n).start()

    pixels = pixels_in[...]
    count = float(TILE * TILE)
    tile_mean = jnp.sum(jnp.sum(pixels, 0, keepdims=True), 1, keepdims=True) / count
    off = pixels - tile_mean
    tile_dev = jnp.sum(jnp.sum(off * off, 0, keepdims=True), 1, keepdims=True)
    row = lax.broadcasted_iota(jnp.int32, (8, 128), 0)
    stat_a[...] = jnp.where(row == 0, tile_mean, tile_dev)
    stats_a[z] = stat_a[...]

    def tell(d, s):
        return copier(stat_a, stats_a.at[z], s.at[abs(d) - 1], sa_r.at[z], {"oy": z + d})

    def heard(d):
        copier(stat_a, stats_a.at[z + d], up_s.at[0], sa_r.at[z + d], {"oy": z + d}).wait_recv()

    for d in range(1, 8):

        @pl.when(z - d >= 0)
        def _(d=d):
            tell(-d, down_s).start()

    loads = [
        pltpu.make_async_copy(src, dst, table_sem.at[k])
        for k, (src, dst) in enumerate(
            ((ix_h, ix), (iy_h, iy), (bx_h, bx), (by_h, by), (ky_h, ky), (kx_h, kx))
        )
    ]
    for load in loads:
        load.start()

    totals = []
    for slot in range(2):
        local = own[part_of(core), :].astype(F32)
        totals.append(jnp.where(a * 8 + j == wanted[slot], 1.0, 0.0) * local)
    for k, copy in enumerate(bank_copies):
        copy.wait()
        d = k + 1 if k < 7 else k - 7
        column = a if k < 7 else partner
        entry = column * 8 + lax.rem(j + 8 - d, 8)
        arrived = bank[k].astype(F32)
        for slot in range(2):
            totals[slot] += jnp.where(entry == wanted[slot], 1.0, 0.0) * arrived
    some_copies = []
    for slot in range(2):
        mine[slot] = totals[slot].astype(BF16)
        for k, peer in enumerate(hi_peers):
            n = slot * 3 + k
            some_copies.append(send(mine.at[slot], some.at[n], some_s.at[n], some_r.at[n], peer))

    def merge(tiles, number):
        means = [t[0:1, :] for t in tiles]
        mid = sum(means) * 0.125
        dev = sum(t[1:2, :] for t in tiles) + number * sum((m - mid) * (m - mid) for m in means)
        return mid, dev

    for copy in across:
        copy.wait()
    for n in range(2):

        @pl.when(sides[n][1])
        def _(n=n):
            corners(n).start()

    for d in range(1, 8):

        @pl.when(z + d < 8)
        def _(d=d):
            heard(d)
            tell(d, up_s).start()

    for d in range(1, 8):

        @pl.when(z - d >= 0)
        def _(d=d):
            heard(-d)

    mid, dev = merge([stats_a.at[k] for k in range(8)], count)
    stat_b[...] = jnp.where(row == 0, mid, dev)
    stat_copies = [
        send(stat_b, stats_b.at[k], sb_s.at[k], sb_r.at[k], peer) for k, peer in enumerate(ox_peers)
    ]

    box_copies = []
    for slot in range(2):
        total = mine[slot].astype(F32)
        for k in range(3):
            some_copies[slot * 3 + k].wait()
            total += some[slot * 3 + k].astype(F32)
        piece[slot] = total.astype(BF16)
        for k, peer in enumerate(box_peers):
            n = slot * 3 + k
            box_copies.append(
                copier(piece.at[slot], boxes.at[n], box_s.at[n], box_r.at[n], peer)
            )
        for k in (2, 1, 0):
            box_copies[slot * 3 + k].start()

    for copy_of in (straight, corners):
        for n in range(2):

            @pl.when(sides[n][1])
            def _(n=n, copy_of=copy_of):
                copy_of(n).wait_send()

            @pl.when(sides[n][2])
            def _(n=n, copy_of=copy_of):
                copy_of(n).wait_recv()

    for r_at, r_size, r_ok in ((0, 256, None), (256, HALF, z < 7), (352, HALF, z > 0)):
        for c_at, c_size, c_ok in ((0, 256, None), (256, 128, a < 7), (384, 128, a > 0)):
            if r_at == 0 and c_at == 0:
                values = pixels_in[...] - tile_mean
            else:
                values = ext[r_at : r_at + r_size, c_at : c_at + c_size] - tile_mean
            for ok in (r_ok, c_ok):
                if ok is not None:
                    values = jnp.where(ok, values, 0.0)
            high, low = split(values)
            ext_hi[r_at : r_at + r_size, c_at : c_at + c_size] = high
            ext_lo[r_at : r_at + r_size, c_at : c_at + c_size] = low

    for load in loads:
        load.wait()

    whole = jnp.concatenate([ext_hi[...], ext_lo[...], ext_hi[...]], axis=1)
    lines = mul(whole, ix[...])
    upper, lower = lines[:FOLD], lines[FOLD:]
    even = mul(iy[0], left_of(upper + lower))
    odd = mul(iy[1], left_of(upper - lower))
    quarter = FOLD // 2
    both = jnp.concatenate([even[:quarter], odd[:quarter], even[quarter:], odd[quarter:]], axis=0)
    for tau in range(2):
        at = slice(tau * 256, tau * 256 + 256)
        image[0, :, at], image[1, :, at] = both_ways(both[:, at])

    y_at = lax.broadcasted_iota(jnp.int32, (TILE, BOX), 0)
    u_at = lax.broadcasted_iota(jnp.int32, (TILE, BOX), 1)
    line = z * TILE + y_at + u_at - HALF
    row_in = jnp.where((line >= 0) & (line < 8 * TILE), 1.0, 0.0).astype(BF16)
    v_at = lax.broadcasted_iota(jnp.int32, (TILE, TILE), 0)
    x_at = lax.broadcasted_iota(jnp.int32, (TILE, TILE), 1)
    line = a * TILE + x_at + v_at - HALF
    col_in = jnp.where((line >= 0) & (line < 8 * TILE) & (v_at < BOX), 1.0, 0.0).astype(BF16)

    out_copies = []
    for slot in range(2):
        for k in range(3):
            box_copies[slot * 3 + k].wait()
        here, there = (
            [first.astype(F32), second.astype(F32)]
            for first, second in (
                (piece[slot], boxes[slot * 3]),
                (boxes[slot * 3 + 1], boxes[slot * 3 + 2]),
            )
        )
        here, there = (
            jnp.concatenate(
                [jnp.where(core == 0, p, q), jnp.where(core == 0, q, p)[2 * PART - ROWS // 2 :]],
                axis=0,
            )
            for p, q in (here, there)
        )
        flat = jnp.concatenate(
            [jnp.where(half == 0, here, there), jnp.where(half == 0, there, here)], axis=0
        )
        tail = flat[BOX:]
        tail = jnp.concatenate([tail, pltpu.roll(tail, 64, 1)], axis=0)
        box = jnp.concatenate([flat[:BOX].astype(BF16), tail.astype(BF16)], axis=1)

        twice = jnp.concatenate([box, box], axis=1)
        wave = mul(by[...], left_of(mul(twice, bx[...])))
        first = lax.broadcasted_iota(jnp.int32, (FOLD, 128), 0) == 0
        joints = []
        for tau in range(2):
            at = slice(tau * 256, tau * 256 + 256)
            t_plus, t_minus = both_ways(wave[:, at])
            p_re, p_im = conj_product(image[0, :, at], t_plus)
            m_re, m_im = conj_product(image[1, :, at], t_minus)
            joint = jnp.concatenate(
                [
                    jnp.concatenate(
                        [p_re + jnp.where(first, 0.0, m_re), p_im + jnp.where(first, 0.0, m_im)],
                        axis=1,
                    ),
                    jnp.concatenate(
                        [jnp.where(first, m_re, m_im - p_im), jnp.where(first, m_im, p_re - m_re)],
                        axis=1,
                    ),
                ],
                axis=0,
            )
            joints.append(joint)
        lines = mul(ky[...], left_of(jnp.concatenate(joints, axis=1)))
        found = mul(left_of(lines, 1), kx[...])
        high, low = split(mul(row_in, box))
        cover = mul(high, col_in) + mul(low, col_in)

        if slot == 0:
            for copy in stat_copies:
                copy.wait()
            mid, dev = merge([stat_b] + [stats_b.at[k] for k in range(7)], count * 8)
            scale = 1.0 / jnp.sqrt(dev[:, 0:1] / (count * 64) + 1e-06)
            rest = mid[:, 0:1] - tile_mean
        corr[slot] = found - rest * cover

        for d in FAR_FIRST:
            to = turn(j, d)
            k = slot * 7 + d - 1
            out_copies.append(
                send(
                    corr.at[slot, pl.ds(pl.multiple_of(to * BAND, BAND), BAND)],
                    got.at[k], out_s.at[k], out_r.at[k], {"ori": to},
                )
            )

    band = pl.ds(pl.multiple_of(j * BAND, BAND), BAND)
    one, two = corr[0, band, :], corr[1, band, :]
    best = jnp.maximum(one, two)
    summed = one + two
    squared = one * one + two * two
    for n, copy in enumerate(out_copies):
        copy.wait()
        value = got[n // 7 * 7 + FAR_FIRST[n % 7] - 1]
        best = jnp.maximum(best, value)
        summed += value
        squared += value * value
    out_ref[0] = best * scale
    out_ref[1] = summed * scale
    out_ref[2] = squared * (scale * scale)
    for d in range(1, 8):

        @pl.when(z - d >= 0)
        def _(d=d):
            tell(-d, down_s).wait_send()

        @pl.when(z + d < 8)
        def _(d=d):
            tell(d, up_s).wait_send()


def body(micrograph, projections, orientations):
    consts = tables()
    vmem = pl.BlockSpec(memory_space=pltpu.VMEM)
    hbm = pl.BlockSpec(memory_space=pl.ANY)
    dma = pltpu.SemaphoreType.DMA
    out = jax.ShapeDtypeStruct((3, BAND, TILE), F32)
    scratch = [
        pltpu.VMEM((TILE, TILE), F32),
        pltpu.VMEM((1, BOX, BOX), BF16),
        pltpu.SMEM((2,), jnp.int32),
        pltpu.VMEM((LEN, 512), F32),
        pltpu.VMEM((LEN, 512), BF16),
        pltpu.VMEM((LEN, 512), BF16),
        pltpu.VMEM((ROWS, 128), BF16),
        pltpu.VMEM((15, PART, 128), BF16),
        pltpu.VMEM((2, PART, 128), BF16),
        pltpu.VMEM((6, PART, 128), BF16),
        pltpu.VMEM((2, PART, 128), BF16),
        pltpu.VMEM((6, PART, 128), BF16),
        pltpu.VMEM((8, 128), F32),
        pltpu.VMEM((8, 8, 128), F32),
        pltpu.VMEM((8, 128), F32),
        pltpu.VMEM((7, 8, 128), F32),
        pltpu.VMEM((2, FOLD, 512), F32),
        pltpu.VMEM((2, TILE, TILE), F32),
        pltpu.VMEM((14, BAND, TILE), F32),
    ]
    scratch += [pltpu.VMEM(c.shape, BF16) for c in consts]
    for n in (3, 6, 6, 6, 15, 15, 6, 6, 6, 6, 7, 7, 8, 7, 7, 14, 14):
        scratch.append(dma((n,)))
    stats = pl.pallas_call(
        kernel,
        out_shape=out,
        in_specs=[hbm] * 9,
        out_specs=vmem,
        scratch_shapes=scratch,
        name="match",
        compiler_params=pltpu.CompilerParams(
            collective_id=0, has_side_effects=True, vmem_limit_bytes=60 * 1024 * 1024
        ),
    )(micrograph, projections, orientations, *[jnp.asarray(c) for c in consts])
    return stats[0], stats[1] / 16.0, stats[2] / 16.0


def solution(mesh):
    in_specs = (P("oy", "ox"), P(("ox", "ori"), None, None), P("ori"))
    out_specs = (P(("oy", "ori"), "ox"), P(("oy", "ori"), "ox"), P(("oy", "ori"), "ox"))
    return jax.shard_map(body, mesh=mesh, in_specs=in_specs, out_specs=out_specs, check_vma=False)
```
